32 devices in a mesh: wide: 4 (over y, x), narrow: 8 (over z, core).
Axes of the slice: x: 2, y: 2, z: 4, core: 2. Of those that a mesh axis runs over, the one named last changes fastest.
Arguments:
- pair_integrals: bfloat16 [65536, 32], P(('wide', 'narrow')), may hold values from -0.0625 to 0.0625
- screening: bfloat16 [32, 32], replicated, may hold values from -1 to 1
- virtual_integrals: bfloat16 [32, 1024, 1024], P(('wide', 'narrow')), may hold values from -0.375 to 0.375
- trials: bfloat16 [1, 256, 1024], P(None, None, 'narrow'), may hold values from -6 to 6
Outputs:
- response: float32 [1024, 1, 256], P('narrow', None, 'wide')
The draws below stay inside these ranges and needn't reach their ends.
All inputs are finite; a program needn't handle non-finite values.
Results may differ from the reference program's by a relative error of at most 0.0041.
Values may be sent and summed in bfloat16 or wider, within the bound.
A program may use at most 64 MiB of HBM per device.

```python
import jax
import jax.numpy as jnp
from jax import lax

O = 256
V = 1024
S = 1
NAUX = 32


def strengthened(values, key, source, target, shards_of, factor):
    def block_of(axis_at):
        return (jnp.arange(values.shape[axis_at]) // (values.shape[axis_at] // shards_of)).reshape((-1,) + (1,) * (values.ndim - 1 - axis_at))

    first = jax.random.permutation(key, shards_of)[block_of(target)]
    second = (block_of(target) + shards_of // 2) % shards_of
    return jnp.where((block_of(source) == first) | (block_of(source) == second), factor * values, values)


def steps_of(stream_key, shape, shards, least, top_value):
    gain, own = 1.0, jax.random.fold_in(stream_key, 6)
    for axis_at, blocks in shards:
        draws = jnp.exp(jax.random.uniform(jax.random.fold_in(own, axis_at), (blocks,), jnp.float32, least / len(shards), top_value / len(shards)))
        gain = gain * jnp.repeat(draws, shape[axis_at] // blocks).reshape([-1 if axis == axis_at else 1 for axis in range(len(shape))])
    return gain


def bell_draw(rng, dims, width, limit, pieces=(), held_as=jnp.bfloat16):
    loudness = steps_of(rng, dims, pieces, -0.22, 0.18) if pieces else 1.0
    drawn = jax.random.normal(rng, dims, jnp.float32) * width * loudness
    return jnp.minimum(jnp.maximum(drawn, -limit), limit).astype(held_as)


def bell_draw_with(stream_key, dims, width, reach, shards, heavy, held_as=jnp.bfloat16):
    values = width * jax.random.normal(stream_key, dims, jnp.float32)
    if shards:
        values = values * steps_of(stream_key, dims, shards, -0.22, 0.18)
    return jnp.clip(strengthened(values, jax.random.fold_in(stream_key, 3), *heavy), -reach, reach).astype(held_as)


def setup_inputs(seed: int = 0) -> dict:
    key_list = jax.random.split(jax.random.key(seed), 5)
    return {
        "pair_integrals": bell_draw(key_list[0], (O * O, NAUX), (O * NAUX) ** -0.5, 0.0625, ((0, 32),)),
        "screening": bell_draw(key_list[1], (NAUX, NAUX), NAUX ** -0.5, 1.0),
        "virtual_integrals": bell_draw_with(key_list[2], (NAUX, V, V), V ** -0.5, 0.375, ((0, 32),), (0, 1, 32, 2.75)),
        "trials": bell_draw(key_list[3], (S, O, V), 1.0, 6.0, ((2, 8),)),
    }


def reference(pair_integrals, screening, virtual_integrals, trials):
    screened = jnp.dot(pair_integrals, screening, preferred_element_type=jnp.float32).astype(jnp.bfloat16)
    trial_rows = trials.astype(jnp.float32).reshape(S * O, V)

    def add_aux(running, inputs):
        slab, column = inputs
        halves = jnp.dot(slab.astype(jnp.float32), trial_rows.T, preferred_element_type=jnp.float32)
        halves = lax.optimization_barrier(halves.astype(jnp.bfloat16)).astype(jnp.float32).reshape(V, S, O)
        tiles = column.astype(jnp.float32).reshape(O, O)
        return running + jnp.einsum("asj,ij->asi", halves, tiles), None

    zeroes = jnp.zeros((V, S, O), jnp.float32)
    response, unused = lax.scan(add_aux, zeroes, (virtual_integrals, screened.T))
    return response
```

```python
import functools

import jax
import jax.numpy as jnp
from jax import lax
from jax.experimental import pallas as pl
from jax.experimental.pallas import tpu as pltpu
from jax.sharding import PartitionSpec as P

LANES = 128
CORES = 2
MESH = pl.DeviceIdType.MESH


def kernel(
    wides, narrows, pairs_ref, screen_ref, virt_ref, trial_ref, out_ref,
    pairs, screen, virt, trial, staged, tiles, tiles_wide, tiles_all, total, halves,
    to_core, from_core, summed, to_wide, from_wide, to_z, from_z,
    local_sem, send_sem, recv_sem,
):
    zs = narrows // CORES
    w, n = lax.axis_index("wide"), lax.axis_index("narrow")
    z, c = lax.div(n, CORES), lax.rem(n, CORES)
    mate = 1 - c
    orbitals = trial.shape[1]
    cut = orbitals // wides
    wide_at = [lax.rem(w + m, wides) for m in range(wides)]
    z_at = [lax.rem(z + k, zs) for k in range(zs)]
    z_from = [lax.rem(z + zs - k, zs) for k in range(zs)]
    narrow_at = [lax.rem(n + m, narrows) for m in range(narrows)]

    barrier = pltpu.get_barrier_semaphore()
    for m in range(1, wides):
        pl.semaphore_signal(barrier, inc=1, device_id={"wide": wide_at[m], "narrow": n}, device_id_type=MESH)
    for m in range(1, narrows):
        pl.semaphore_signal(barrier, inc=1, device_id={"wide": w, "narrow": narrow_at[m]}, device_id_type=MESH)

    sent = []

    def send(source, target, wide, narrow):
        at = len(sent)
        copy = pltpu.make_async_remote_copy(
            src_ref=source, dst_ref=target, send_sem=send_sem.at[at], recv_sem=recv_sem.at[at],
            device_id={"wide": wide, "narrow": narrow}, device_id_type=MESH,
        )
        copy.start()
        sent.append(copy)
        return copy

    def fetch(source, target, at):
        copy = pltpu.make_async_copy(source, target, local_sem.at[at])
        copy.start()
        return copy

    get_pairs = fetch(pairs_ref, pairs, 0)
    get_screen = fetch(screen_ref, screen, 1)
    get_trial = fetch(trial_ref, trial.at[n], 2)
    depth = virt.shape[2]
    get_virt = [
        fetch(virt_ref.at[:, pl.ds(pl.multiple_of(z_from[k] * depth, depth), depth)], virt.at[k], 3 + k)
        for k in range(zs)
    ]

    get_pairs.wait()
    get_screen.wait()
    product = lax.dot_general(
        screen[...], pairs[...], (((0,), (0,)), ((), ())), preferred_element_type=jnp.float32
    )
    aux = wides * narrows
    rows = tiles.shape[2]
    halves_j = orbitals // LANES
    own_i = rows // halves_j
    for i in range(own_i):
        for h in range(halves_j):
            t = i * halves_j + h
            staged[pl.ds(h * own_i + i, aux, stride=rows), :] = product[:, t * LANES : (t + 1) * LANES]
    tiles[...] = staged[...].reshape(tiles.shape).astype(jnp.bfloat16)
    tiles_wide[w] = tiles[w]
    get_trial.wait()

    pl.semaphore_wait(barrier, wides + narrows - 2)

    def share(block, of):
        return trial.at[block, pl.ds(pl.multiple_of(of * cut, cut), cut)]

    along_z = {k: send(share(n, w), share(n, w), w, z_at[k] * CORES + c) for k in range(zs - 1, 0, -1)}
    to_mate = send(trial.at[n], trial.at[n], w, z * CORES + mate)
    tiles_in = [send(tiles.at[wide_at[m]], tiles_wide.at[w], wide_at[m], n) for m in range(1, wides)]

    def chunk(k):
        first = z_from[k] * CORES
        wide_rows = jnp.concatenate([trial[first + p] for p in range(CORES)], axis=1)
        return lax.dot_general(
            wide_rows, virt[k], (((1,), (1,)), ((), ())), preferred_element_type=jnp.float32
        )

    get_virt[0].wait()
    to_mate.wait_recv()
    total[...] = chunk(0)

    across = {}
    for k in range(1, zs):
        along_z[k].wait_recv()
        block = z_from[k] * CORES + c
        across[k] = [send(share(block, w), share(block, w), wide_at[m], n) for m in range(1, wides)]

    for copy in tiles_in:
        copy.wait_recv()
    tiles_all[n] = tiles_wide[:, n]
    tiles_done = [
        send(tiles_wide.at[:, narrow_at[m]], tiles_all.at[n], w, narrow_at[m]) for m in range(1, narrows)
    ]

    relayed = {}
    for k in range(1, zs):
        for copy in across[k]:
            copy.wait_recv()
        block = z_from[k] * CORES + c
        relayed[k] = send(trial.at[block], trial.at[block], w, z * CORES + mate)
    for k in range(1, zs):
        get_virt[k].wait()
        relayed[k].wait_recv()
        total[...] += chunk(k)
    for b in range(narrows):
        halves[b] = total[:, b * LANES : (b + 1) * LANES].astype(jnp.bfloat16)

    for copy in tiles_done:
        copy.wait_recv()
    columns = []
    for h in range(halves_j):
        parts = [
            tiles_all[b, a].astype(jnp.float32)[h * own_i : (h + 1) * own_i]
            for a in range(wides)
            for b in range(narrows)
        ]
        columns.append(jnp.concatenate(parts, axis=0))
    screened = jnp.concatenate(columns, axis=1).astype(jnp.bfloat16)

    order = list(range(1, zs)) + [0]
    from_mate, from_wides, from_zs = {}, {}, {}
    for k in order:
        to_core[k] = jnp.dot(
            screened, halves[z_at[k] * CORES + mate], preferred_element_type=jnp.float32
        ).astype(jnp.bfloat16)
        from_mate[k] = send(to_core.at[k], from_core.at[k], w, z * CORES + mate)
    for k in order:
        own = jnp.dot(screened, halves[z_at[k] * CORES + c], preferred_element_type=jnp.float32)
        from_mate[k].wait_recv()
        value = own + from_core[k].astype(jnp.float32)
        summed[k] = value
        to_wide[k] = value.astype(jnp.bfloat16)
        from_wides[k] = [
            send(
                to_wide.at[k, pl.ds(pl.multiple_of(wide_at[m] * cut, cut), cut)],
                from_wide.at[k, m - 1], wide_at[m], n,
            )
            for m in range(1, wides)
        ]
    for k in order:
        value = summed[k, pl.ds(pl.multiple_of(w * cut, cut), cut), :]
        for m in range(1, wides):
            from_wides[k][m - 1].wait_recv()
            value = value + from_wide[k, m - 1].astype(jnp.float32)
        if k:
            to_z[k - 1] = value.astype(jnp.bfloat16)
            from_zs[k] = send(to_z.at[k - 1], from_z.at[k - 1], w, z_at[k] * CORES + c)
    for k in range(1, zs):
        from_zs[k].wait_recv()
        value = value + from_z[k - 1].astype(jnp.float32)
    out_ref[...] = value
    for copy in sent:
        copy.wait_send()


def fused(wides, narrows, pair_integrals, screening, virtual_integrals, trials):
    zs = narrows // CORES
    orbitals, columns = trials.shape[1:]
    virtuals = virtual_integrals.shape[1]
    aux = screening.shape[1]
    pairs_here = pair_integrals.shape[0]
    rows = pairs_here // LANES
    cut = orbitals // wides
    bf, f4 = jnp.bfloat16, jnp.float32
    copies = (zs - 1) * 2 + 1 + (zs - 1) * (wides - 1) + (wides - 1) + (narrows - 1)
    copies += zs + zs * (wides - 1) + (zs - 1)
    anywhere = pl.BlockSpec(memory_space=pl.ANY)
    out = pl.pallas_call(
        functools.partial(kernel, wides, narrows),
        out_shape=jax.ShapeDtypeStruct((cut, columns), f4),
        in_specs=[anywhere] * 4,
        out_specs=pl.BlockSpec(memory_space=pltpu.VMEM),
        scratch_shapes=[
            pltpu.VMEM((aux, pairs_here), bf),
            pltpu.VMEM(screening.shape, bf),
            pltpu.VMEM((zs, virtuals, virtuals // zs), bf),
            pltpu.VMEM((narrows, orbitals, columns), bf),
            pltpu.VMEM((aux * rows, LANES), f4),
            pltpu.VMEM((wides, narrows, rows, LANES), bf),
            pltpu.VMEM((wides, narrows, rows, LANES), bf),
            pltpu.VMEM((narrows, wides, rows, LANES), bf),
            pltpu.VMEM((orbitals, virtuals), f4),
            pltpu.VMEM((narrows, orbitals, columns), bf),
            pltpu.VMEM((zs, orbitals, columns), bf),
            pltpu.VMEM((zs, orbitals, columns), bf),
            pltpu.VMEM((zs, orbitals, columns), f4),
            pltpu.VMEM((zs, orbitals, columns), bf),
            pltpu.VMEM((zs, wides - 1, cut, columns), bf),
            pltpu.VMEM((zs - 1, cut, columns), bf),
            pltpu.VMEM((zs - 1, cut, columns), bf),
            pltpu.SemaphoreType.DMA((3 + zs,)),
            pltpu.SemaphoreType.DMA((copies,)),
            pltpu.SemaphoreType.DMA((copies,)),
        ],
        compiler_params=pltpu.CompilerParams(
            collective_id=0, has_side_effects=True, vmem_limit_bytes=48 * 2**20
        ),
    )(pair_integrals.T, screening, virtual_integrals[0], trials[0])
    return out.T[:, None, :]


def plain(pair_integrals, screening, virtual_integrals, trials):
    orbitals = trials.shape[1]
    screened = jnp.dot(pair_integrals, screening, preferred_element_type=jnp.float32).astype(
        jnp.bfloat16
    )
    blocks = screened.reshape((1, 1) + screened.shape)
    owned_tiles = lax.all_to_all(
        lax.all_to_all(blocks, "wide", split_axis=3, concat_axis=0, tiled=True),
        "narrow",
        split_axis=3,
        concat_axis=1,
        tiled=True,
    )
    pair_tiles = owned_tiles.reshape(orbitals, orbitals, owned_tiles.shape[3])
    whole_trials = lax.all_gather(trials, "narrow", axis=2, tiled=True)
    halves = jnp.einsum(
        "qab,sjb->qasj", virtual_integrals, whole_trials, preferred_element_type=jnp.float32
    ).astype(jnp.bfloat16)
    shares = lax.psum_scatter(
        jnp.einsum("qasj,ijq->asi", halves, pair_tiles, preferred_element_type=jnp.float32),
        "narrow",
        scatter_dimension=0,
        tiled=True,
    )
    return lax.psum_scatter(shares, "wide", scatter_dimension=2, tiled=True)


def per_device(wides, narrows, pair_integrals, screening, virtual_integrals, trials):
    trial_count, orbitals, columns = trials.shape
    own_i = pair_integrals.shape[0] // orbitals
    fits = (
        trial_count == 1
        and virtual_integrals.shape[0] == 1
        and screening.shape[1] == wides * narrows
        and columns == LANES
        and orbitals % LANES == 0
        and orbitals % (16 * wides) == 0
        and narrows % CORES == 0
        and own_i % 8 == 0
        and (own_i * orbitals // LANES) % 16 == 0
    )
    if fits:
        return fused(wides, narrows, pair_integrals, screening, virtual_integrals, trials)
    return plain(pair_integrals, screening, virtual_integrals, trials)


def solution(mesh):
    return jax.shard_map(
        functools.partial(per_device, mesh.shape["wide"], mesh.shape["narrow"]),
        mesh=mesh,
        in_specs=(
            P(("wide", "narrow"), None),
            P(),
            P(("wide", "narrow"), None, None),
            P(None, None, "narrow"),
        ),
        out_specs=P("narrow", None, "wide"),
        check_vma=False,
    )
```

```python
import functools

import jax
import jax.numpy as jnp
from jax import lax
from jax.experimental import pallas as pl
from jax.experimental.pallas import tpu as pltpu
from jax.sharding import PartitionSpec as P

LANES = 128
CORES = 2
MESH = pl.DeviceIdType.MESH


def kernel(
    wides, narrows, pairs_ref, screen_ref, virt_ref, trial_ref, out_ref,
    pairs, screen, virt, trial, staged, tiles, tiles_wide, tiles_all, total, halves,
    to_core, from_core, summed, to_wide, from_wide, to_z, from_z,
    local_sem, send_sem, recv_sem,
):
    zs = narrows // CORES
    w, n = lax.axis_index("wide"), lax.axis_index("narrow")
    z, c = lax.div(n, CORES), lax.rem(n, CORES)
    mate = 1 - c
    orbitals = trial.shape[1]
    cut = orbitals // wides
    wide_at = [lax.rem(w + m, wides) for m in range(wides)]
    z_at = [lax.rem(z + k, zs) for k in range(zs)]
    z_from = [lax.rem(z + zs - k, zs) for k in range(zs)]
    narrow_at = [lax.rem(n + m, narrows) for m in range(narrows)]

    barrier = pltpu.get_barrier_semaphore()
    for m in range(1, wides):
        pl.semaphore_signal(barrier, inc=1, device_id={"wide": wide_at[m], "narrow": n}, device_id_type=MESH)
    for m in range(1, narrows):
        pl.semaphore_signal(barrier, inc=1, device_id={"wide": w, "narrow": narrow_at[m]}, device_id_type=MESH)

    sent = []

    def send(source, target, wide, narrow):
        at = len(sent)
        copy = pltpu.make_async_remote_copy(
            src_ref=source, dst_ref=target, send_sem=send_sem.at[at], recv_sem=recv_sem.at[at],
            device_id={"wide": wide, "narrow": narrow}, device_id_type=MESH,
        )
        copy.start()
        sent.append(copy)
        return copy

    def fetch(source, target, at):
        copy = pltpu.make_async_copy(source, target, local_sem.at[at])
        copy.start()
        return copy

    get_pairs = fetch(pairs_ref, pairs, 0)
    get_screen = fetch(screen_ref, screen, 1)
    get_trial = fetch(trial_ref, trial.at[n], 2)
    depth = virt.shape[2]
    get_virt = [
        fetch(virt_ref.at[:, pl.ds(pl.multiple_of(z_from[k] * depth, depth), depth)], virt.at[k], 3 + k)
        for k in range(zs)
    ]

    pl.semaphore_wait(barrier, wides + narrows - 2)

    def share(block, of):
        return trial.at[block, pl.ds(pl.multiple_of(of * cut, cut), cut)]

    mine = trial_ref.at[pl.ds(pl.multiple_of(w * cut, cut), cut)]
    along_z = {k: send(mine, share(n, w), w, z_at[k] * CORES + c) for k in range(1, zs)}
    to_mate = send(trial_ref, trial.at[n], w, z * CORES + mate)

    get_pairs.wait()
    get_screen.wait()
    product = lax.dot_general(
        screen[...], pairs[...], (((0,), (0,)), ((), ())), preferred_element_type=jnp.float32
    )
    aux = wides * narrows
    rows = tiles.shape[2]
    halves_j = orbitals // LANES
    own_i = rows // halves_j
    for i in range(own_i):
        for h in range(halves_j):
            t = i * halves_j + h
            staged[pl.ds(h * own_i + i, aux, stride=rows), :] = product[:, t * LANES : (t + 1) * LANES]
    tiles[...] = staged[...].reshape(tiles.shape).astype(jnp.bfloat16)
    tiles_wide[w] = tiles[w]
    tiles_in = [send(tiles.at[wide_at[m]], tiles_wide.at[w], wide_at[m], n) for m in range(1, wides)]

    def chunk(k):
        first = z_from[k] * CORES
        wide_rows = jnp.concatenate([trial[first + p] for p in range(CORES)], axis=1)
        return lax.dot_general(
            wide_rows, virt[k], (((1,), (1,)), ((), ())), preferred_element_type=jnp.float32
        )

    get_trial.wait()
    get_virt[0].wait()
    to_mate.wait_recv()
    total[...] = chunk(0)

    across = {}
    for k in range(1, zs):
        along_z[k].wait_recv()
        block = z_from[k] * CORES + c
        across[k] = [send(share(block, w), share(block, w), wide_at[m], n) for m in range(1, wides)]

    for copy in tiles_in:
        copy.wait_recv()
    tiles_all[n] = tiles_wide[:, n]
    tiles_done = [
        send(tiles_wide.at[:, narrow_at[m]], tiles_all.at[n], w, narrow_at[m]) for m in range(1, narrows)
    ]

    relayed = {}
    for k in range(1, zs):
        for copy in across[k]:
            copy.wait_recv()
        block = z_from[k] * CORES + c
        relayed[k] = send(trial.at[block], trial.at[block], w, z * CORES + mate)
    for k in range(1, zs - 1):
        get_virt[k].wait()
        relayed[k].wait_recv()
        total[...] += chunk(k)

    for copy in tiles_done:
        copy.wait_recv()
    columns = []
    for h in range(halves_j):
        parts = [
            tiles_all[b, a].astype(jnp.float32)[h * own_i : (h + 1) * own_i]
            for a in range(wides)
            for b in range(narrows)
        ]
        columns.append(jnp.concatenate(parts, axis=0))
    screened = jnp.concatenate(columns, axis=1).astype(jnp.bfloat16)

    get_virt[zs - 1].wait()
    relayed[zs - 1].wait_recv()
    whole = (total[...] + chunk(zs - 1)).astype(jnp.bfloat16)
    for b in range(narrows):
        halves[b] = whole[:, b * LANES : (b + 1) * LANES]

    order = list(range(1, zs)) + [0]
    from_mate, from_wides, from_zs = {}, {}, {}
    for k in order:
        to_core[k] = jnp.dot(
            screened, halves[z_at[k] * CORES + mate], preferred_element_type=jnp.float32
        ).astype(jnp.bfloat16)
        from_mate[k] = send(to_core.at[k], from_core.at[k], w, z * CORES + mate)
    for k in order:
        own = jnp.dot(screened, halves[z_at[k] * CORES + c], preferred_element_type=jnp.float32)
        from_mate[k].wait_recv()
        value = own + from_core[k].astype(jnp.float32)
        summed[k] = value
        to_wide[k] = value.astype(jnp.bfloat16)
        from_wides[k] = [
            send(
                to_wide.at[k, pl.ds(pl.multiple_of(wide_at[m] * cut, cut), cut)],
                from_wide.at[k, m - 1], wide_at[m], n,
            )
            for m in range(1, wides)
        ]
    for k in order:
        value = summed[k, pl.ds(pl.multiple_of(w * cut, cut), cut), :]
        for m in range(1, wides):
            from_wides[k][m - 1].wait_recv()
            value = value + from_wide[k, m - 1].astype(jnp.float32)
        if k:
            to_z[k - 1] = value.astype(jnp.bfloat16)
            from_zs[k] = send(to_z.at[k - 1], from_z.at[k - 1], w, z_at[k] * CORES + c)
    for k in range(1, zs):
        from_zs[k].wait_recv()
        value = value + from_z[k - 1].astype(jnp.float32)
    out_ref[...] = value
    for copy in sent:
        copy.wait_send()


def fused(wides, narrows, pair_integrals, screening, virtual_integrals, trials):
    zs = narrows // CORES
    orbitals, columns = trials.shape[1:]
    virtuals = virtual_integrals.shape[1]
    aux = screening.shape[1]
    pairs_here = pair_integrals.shape[0]
    rows = pairs_here // LANES
    cut = orbitals // wides
    bf, f4 = jnp.bfloat16, jnp.float32
    copies = (zs - 1) * 2 + 1 + (zs - 1) * (wides - 1) + (wides - 1) + (narrows - 1)
    copies += zs + zs * (wides - 1) + (zs - 1)
    anywhere = pl.BlockSpec(memory_space=pl.ANY)
    out = pl.pallas_call(
        functools.partial(kernel, wides, narrows),
        out_shape=jax.ShapeDtypeStruct((cut, columns), f4),
        in_specs=[anywhere] * 4,
        out_specs=pl.BlockSpec(memory_space=pltpu.VMEM),
        scratch_shapes=[
            pltpu.VMEM((aux, pairs_here), bf),
            pltpu.VMEM(screening.shape, bf),
            pltpu.VMEM((zs, virtuals, virtuals // zs), bf),
            pltpu.VMEM((narrows, orbitals, columns), bf),
            pltpu.VMEM((aux * rows, LANES), f4),
            pltpu.VMEM((wides, narrows, rows, LANES), bf),
            pltpu.VMEM((wides, narrows, rows, LANES), bf),
            pltpu.VMEM((narrows, wides, rows, LANES), bf),
            pltpu.VMEM((orbitals, virtuals), f4),
            pltpu.VMEM((narrows, orbitals, columns), bf),
            pltpu.VMEM((zs, orbitals, columns), bf),
            pltpu.VMEM((zs, orbitals, columns), bf),
            pltpu.VMEM((zs, orbitals, columns), f4),
            pltpu.VMEM((zs, orbitals, columns), bf),
            pltpu.VMEM((zs, wides - 1, cut, columns), bf),
            pltpu.VMEM((zs - 1, cut, columns), bf),
            pltpu.VMEM((zs - 1, cut, columns), bf),
            pltpu.SemaphoreType.DMA((3 + zs,)),
            pltpu.SemaphoreType.DMA((copies,)),
            pltpu.SemaphoreType.DMA((copies,)),
        ],
        compiler_params=pltpu.CompilerParams(
            collective_id=0, has_side_effects=True, vmem_limit_bytes=60 * 2**20
        ),
    )(pair_integrals.T, screening, virtual_integrals[0], trials[0])
    return out.T[:, None, :]


def plain(pair_integrals, screening, virtual_integrals, trials):
    orbitals = trials.shape[1]
    screened = jnp.dot(pair_integrals, screening, preferred_element_type=jnp.float32).astype(
        jnp.bfloat16
    )
    blocks = screened.reshape((1, 1) + screened.shape)
    owned_tiles = lax.all_to_all(
        lax.all_to_all(blocks, "wide", split_axis=3, concat_axis=0, tiled=True),
        "narrow",
        split_axis=3,
        concat_axis=1,
        tiled=True,
    )
    pair_tiles = owned_tiles.reshape(orbitals, orbitals, owned_tiles.shape[3])
    whole_trials = lax.all_gather(trials, "narrow", axis=2, tiled=True)
    halves = jnp.einsum(
        "qab,sjb->qasj", virtual_integrals, whole_trials, preferred_element_type=jnp.float32
    ).astype(jnp.bfloat16)
    shares = lax.psum_scatter(
        jnp.einsum("qasj,ijq->asi", halves, pair_tiles, preferred_element_type=jnp.float32),
        "narrow",
        scatter_dimension=0,
        tiled=True,
    )
    return lax.psum_scatter(shares, "wide", scatter_dimension=2, tiled=True)


def per_device(wides, narrows, pair_integrals, screening, virtual_integrals, trials):
    trial_count, orbitals, columns = trials.shape
    own_i = pair_integrals.shape[0] // orbitals
    fits = (
        trial_count == 1
        and virtual_integrals.shape[0] == 1
        and screening.shape[1] == wides * narrows
        and columns == LANES
        and orbitals % LANES == 0
        and orbitals % (16 * wides) == 0
        and narrows % CORES == 0
        and own_i % 8 == 0
        and (own_i * orbitals // LANES) % 16 == 0
    )
    if fits:
        return fused(wides, narrows, pair_integrals, screening, virtual_integrals, trials)
    return plain(pair_integrals, screening, virtual_integrals, trials)


def solution(mesh):
    return jax.shard_map(
        functools.partial(per_device, mesh.shape["wide"], mesh.shape["narrow"]),
        mesh=mesh,
        in_specs=(
            P(("wide", "narrow"), None),
            P(),
            P(("wide", "narrow"), None, None),
            P(None, None, "narrow"),
        ),
        out_specs=P("narrow", None, "wide"),
        check_vma=False,
    )
```

```python
import functools

import jax
import jax.numpy as jnp
from jax import lax
from jax.experimental import pallas as pl
from jax.experimental.pallas import tpu as pltpu
from jax.sharding import PartitionSpec as P

LANES = 128
CORES = 2
MESH = pl.DeviceIdType.MESH


def flipped(index, mask):
    bit = 1
    result = index
    while bit <= mask:
        if mask & bit:
            result = result + bit * (1 - 2 * lax.rem(lax.div(index, bit), 2))
        bit *= 2
    return result


def kernel(
    wides, narrows, pairs_ref, screen_ref, virt_ref, trial_ref, out_ref,
    pairs, screen, virt, trial, staged, tiles, tiles_wide, tiles_all, total, halves,
    to_core, from_core, summed, to_wide, from_wide, to_z, from_z,
    local_sem, send_sem, recv_sem,
):
    zs = narrows // CORES
    w, n = lax.axis_index("wide"), lax.axis_index("narrow")
    z, c = lax.div(n, CORES), lax.rem(n, CORES)
    mate = 1 - c
    orbitals = trial.shape[1]
    cut = orbitals // wides
    wide_at = [flipped(w, m) for m in range(wides)]
    z_at = [flipped(z, k) for k in range(zs)]
    narrow_at = [flipped(n, m) for m in range(narrows)]
    wide_order = [wides - 1] + list(range(1, wides - 1))

    barrier = pltpu.get_barrier_semaphore()
    for m in range(1, wides):
        pl.semaphore_signal(barrier, inc=1, device_id={"wide": wide_at[m], "narrow": n}, device_id_type=MESH)
    for m in range(1, narrows):
        pl.semaphore_signal(barrier, inc=1, device_id={"wide": w, "narrow": narrow_at[m]}, device_id_type=MESH)

    sent = []

    def send(source, target, wide, narrow):
        at = len(sent)
        copy = pltpu.make_async_remote_copy(
            src_ref=source, dst_ref=target, send_sem=send_sem.at[at], recv_sem=recv_sem.at[at],
            device_id={"wide": wide, "narrow": narrow}, device_id_type=MESH,
        )
        copy.start()
        sent.append(copy)
        return copy

    def fetch(source, target, at):
        copy = pltpu.make_async_copy(source, target, local_sem.at[at])
        copy.start()
        return copy

    get_pairs = fetch(pairs_ref, pairs, 0)
    get_screen = fetch(screen_ref, screen, 1)
    get_trial = fetch(trial_ref, trial.at[n], 2)
    depth = virt.shape[2]
    get_virt = [
        fetch(virt_ref.at[:, pl.ds(pl.multiple_of(z_at[k] * depth, depth), depth)], virt.at[k], 3 + k)
        for k in range(zs)
    ]

    pl.semaphore_wait(barrier, wides + narrows - 2)

    def share(block, of):
        return trial.at[block, pl.ds(pl.multiple_of(of * cut, cut), cut)]

    mine = trial_ref.at[pl.ds(pl.multiple_of(w * cut, cut), cut)]
    along_z = {k: send(mine, share(n, w), w, z_at[k] * CORES + c) for k in range(1, zs)}
    to_mate = send(trial_ref, trial.at[n], w, z * CORES + mate)

    get_pairs.wait()
    get_screen.wait()
    product = lax.dot_general(
        screen[...], pairs[...], (((0,), (0,)), ((), ())), preferred_element_type=jnp.float32
    )
    aux = wides * narrows
    rows = tiles.shape[2]
    halves_j = orbitals // LANES
    own_i = rows // halves_j
    for i in range(own_i):
        for h in range(halves_j):
            t = i * halves_j + h
            staged[pl.ds(h * own_i + i, aux, stride=rows), :] = product[:, t * LANES : (t + 1) * LANES]
    tiles[...] = staged[...].reshape(tiles.shape).astype(jnp.bfloat16)
    tiles_wide[w] = tiles[w]
    tiles_in = [send(tiles.at[wide_at[m]], tiles_wide.at[w], wide_at[m], n) for m in wide_order]

    def chunk(k):
        first = z_at[k] * CORES
        wide_rows = jnp.concatenate([trial[first + p] for p in range(CORES)], axis=1)
        return lax.dot_general(
            wide_rows, virt[k], (((1,), (1,)), ((), ())), preferred_element_type=jnp.float32
        )

    get_trial.wait()
    get_virt[0].wait()
    to_mate.wait_recv()
    total[...] = chunk(0)

    across = {}
    for k in range(1, zs):
        along_z[k].wait_recv()
        block = z_at[k] * CORES + c
        across[k] = [send(share(block, w), share(block, w), wide_at[m], n) for m in wide_order]

    for copy in tiles_in:
        copy.wait_recv()
    tiles_all[n] = tiles_wide[:, n]
    tiles_done = [
        send(tiles_wide.at[:, narrow_at[m]], tiles_all.at[n], w, narrow_at[m]) for m in range(1, narrows)
    ]

    relayed = {}
    for k in range(1, zs):
        for copy in across[k]:
            copy.wait_recv()
        block = z_at[k] * CORES + c
        relayed[k] = send(trial.at[block], trial.at[block], w, z * CORES + mate)
    for k in range(1, zs - 1):
        get_virt[k].wait()
        relayed[k].wait_recv()
        total[...] += chunk(k)

    for copy in tiles_done:
        copy.wait_recv()
    columns = []
    for h in range(halves_j):
        parts = [
            tiles_all[b, a].astype(jnp.float32)[h * own_i : (h + 1) * own_i]
            for a in range(wides)
            for b in range(narrows)
        ]
        columns.append(jnp.concatenate(parts, axis=0))
    screened = jnp.concatenate(columns, axis=1).astype(jnp.bfloat16)

    get_virt[zs - 1].wait()
    relayed[zs - 1].wait_recv()
    whole = (total[...] + chunk(zs - 1)).astype(jnp.bfloat16)
    for b in range(narrows):
        halves[b] = whole[:, b * LANES : (b + 1) * LANES]

    order = list(range(zs - 1, -1, -1))
    from_mate, from_wides, from_zs = {}, {}, {}
    for k in order:
        to_core[k] = jnp.dot(
            screened, halves[z_at[k] * CORES + mate], preferred_element_type=jnp.float32
        ).astype(jnp.bfloat16)
        from_mate[k] = send(to_core.at[k], from_core.at[k], w, z * CORES + mate)
    early = len(sent)
    for k in order:
        own = jnp.dot(screened, halves[z_at[k] * CORES + c], preferred_element_type=jnp.float32)
        from_mate[k].wait_recv()
        value = own + from_core[k].astype(jnp.float32)
        summed[k] = value
        to_wide[k] = value.astype(jnp.bfloat16)
        from_wides[k] = [
            send(
                to_wide.at[k, pl.ds(pl.multiple_of(wide_at[m] * cut, cut), cut)],
                from_wide.at[k, m - 1], wide_at[m], n,
            )
            for m in wide_order
        ]
    for copy in sent[:early]:
        copy.wait_send()
    for k in order:
        value = summed[k, pl.ds(pl.multiple_of(w * cut, cut), cut), :]
        for copy in from_wides[k]:
            copy.wait_recv()
        for m in range(1, wides):
            value = value + from_wide[k, m - 1].astype(jnp.float32)
        if k:
            to_z[k - 1] = value.astype(jnp.bfloat16)
            from_zs[k] = send(to_z.at[k - 1], from_z.at[k - 1], w, z_at[k] * CORES + c)
    for copy in sent[early : early + zs * (wides - 1)]:
        copy.wait_send()
    for k in range(1, zs):
        from_zs[k].wait_recv()
        value = value + from_z[k - 1].astype(jnp.float32)
    out_ref[...] = value
    for copy in sent[early + zs * (wides - 1) :]:
        copy.wait_send()


def fused(wides, narrows, pair_integrals, screening, virtual_integrals, trials):
    zs = narrows // CORES
    orbitals, columns = trials.shape[1:]
    virtuals = virtual_integrals.shape[1]
    aux = screening.shape[1]
    pairs_here = pair_integrals.shape[0]
    rows = pairs_here // LANES
    cut = orbitals // wides
    bf, f4 = jnp.bfloat16, jnp.float32
    copies = (zs - 1) * 2 + 1 + (zs - 1) * (wides - 1) + (wides - 1) + (narrows - 1)
    copies += zs + zs * (wides - 1) + (zs - 1)
    anywhere = pl.BlockSpec(memory_space=pl.ANY)
    operands = (pair_integrals.T, screening, virtual_integrals[0], trials[0])
    out = pl.pallas_call(
        functools.partial(kernel, wides, narrows),
        out_shape=jax.ShapeDtypeStruct((cut, columns), f4),
        in_specs=[anywhere] * 4,
        out_specs=pl.BlockSpec(memory_space=pltpu.VMEM),
        scratch_shapes=[
            pltpu.VMEM((aux, pairs_here), bf),
            pltpu.VMEM(screening.shape, bf),
            pltpu.VMEM((zs, virtuals, virtuals // zs), bf),
            pltpu.VMEM((narrows, orbitals, columns), bf),
            pltpu.VMEM((aux * rows, LANES), f4),
            pltpu.VMEM((wides, narrows, rows, LANES), bf),
            pltpu.VMEM((wides, narrows, rows, LANES), bf),
            pltpu.VMEM((narrows, wides, rows, LANES), bf),
            pltpu.VMEM((orbitals, virtuals), f4),
            pltpu.VMEM((narrows, orbitals, columns), bf),
            pltpu.VMEM((zs, orbitals, columns), bf),
            pltpu.VMEM((zs, orbitals, columns), bf),
            pltpu.VMEM((zs, orbitals, columns), f4),
            pltpu.VMEM((zs, orbitals, columns), bf),
            pltpu.VMEM((zs, wides - 1, cut, columns), bf),
            pltpu.VMEM((zs - 1, cut, columns), bf),
            pltpu.VMEM((zs - 1, cut, columns), bf),
            pltpu.SemaphoreType.DMA((3 + zs,)),
            pltpu.SemaphoreType.DMA((copies,)),
            pltpu.SemaphoreType.DMA((copies,)),
        ],
        compiler_params=pltpu.CompilerParams(
            collective_id=0, has_side_effects=True, vmem_limit_bytes=32 * 2**20
        ),
    )(*[pltpu.with_memory_space_constraint(x, pltpu.HBM) for x in operands])
    return out.T[:, None, :]


def plain(pair_integrals, screening, virtual_integrals, trials):
    orbitals = trials.shape[1]
    screened = jnp.dot(pair_integrals, screening, preferred_element_type=jnp.float32).astype(
        jnp.bfloat16
    )
    blocks = screened.reshape((1, 1) + screened.shape)
    owned_tiles = lax.all_to_all(
        lax.all_to_all(blocks, "wide", split_axis=3, concat_axis=0, tiled=True),
        "narrow",
        split_axis=3,
        concat_axis=1,
        tiled=True,
    )
    pair_tiles = owned_tiles.reshape(orbitals, orbitals, owned_tiles.shape[3])
    whole_trials = lax.all_gather(trials, "narrow", axis=2, tiled=True)
    halves = jnp.einsum(
        "qab,sjb->qasj", virtual_integrals, whole_trials, preferred_element_type=jnp.float32
    ).astype(jnp.bfloat16)
    shares = lax.psum_scatter(
        jnp.einsum("qasj,ijq->asi", halves, pair_tiles, preferred_element_type=jnp.float32),
        "narrow",
        scatter_dimension=0,
        tiled=True,
    )
    return lax.psum_scatter(shares, "wide", scatter_dimension=2, tiled=True)


def per_device(wides, narrows, pair_integrals, screening, virtual_integrals, trials):
    trial_count, orbitals, columns = trials.shape
    own_i = pair_integrals.shape[0] // orbitals
    fits = (
        trial_count == 1
        and virtual_integrals.shape[0] == 1
        and screening.shape[1] == wides * narrows
        and columns == LANES
        and orbitals % LANES == 0
        and orbitals % (16 * wides) == 0
        and narrows % CORES == 0
        and wides & (wides - 1) == 0
        and narrows & (narrows - 1) == 0
        and wides > 1
        and narrows > CORES
        and own_i % 8 == 0
        and (own_i * orbitals // LANES) % 16 == 0
    )
    if fits:
        return fused(wides, narrows, pair_integrals, screening, virtual_integrals, trials)
    return plain(pair_integrals, screening, virtual_integrals, trials)


def solution(mesh):
    return jax.shard_map(
        functools.partial(per_device, mesh.shape["wide"], mesh.shape["narrow"]),
        mesh=mesh,
        in_specs=(
            P(("wide", "narrow"), None),
            P(),
            P(("wide", "narrow"), None, None),
            P(None, None, "narrow"),
        ),
        out_specs=P("narrow", None, "wide"),
        check_vma=False,
    )
```

```python
import functools

import jax
import jax.numpy as jnp
from jax import lax
from jax.experimental import pallas as pl
from jax.experimental.pallas import tpu as pltpu
from jax.sharding import PartitionSpec as P

LANES = 128
CORES = 2
MESH = pl.DeviceIdType.MESH


def flipped(index, mask):
    bit = 1
    result = index
    while bit <= mask:
        if mask & bit:
            result = result + bit * (1 - 2 * lax.rem(lax.div(index, bit), 2))
        bit *= 2
    return result


def kernel(
    wides, narrows, pairs_ref, screen_ref, virt_ref, trial_ref, out_ref,
    pairs, screen, virt, trial, staged, tiles, tiles_wide, tiles_all, total, partial,
    to_core, from_core, summed, to_wide, from_wide, to_z, from_z,
    local_sem, send_sem, recv_sem,
):
    zs = narrows // CORES
    w, n = lax.axis_index("wide"), lax.axis_index("narrow")
    z, c = lax.div(n, CORES), lax.rem(n, CORES)
    mate = 1 - c
    orbitals = trial.shape[1]
    cut = orbitals // wides
    wide_at = [flipped(w, m) for m in range(wides)]
    z_at = [flipped(z, k) for k in range(zs)]
    narrow_at = [flipped(n, m) for m in range(narrows)]
    wide_order = [wides - 1] + list(range(1, wides - 1))

    barrier = pltpu.get_barrier_semaphore()
    for m in range(1, wides):
        pl.semaphore_signal(barrier, inc=1, device_id={"wide": wide_at[m], "narrow": n}, device_id_type=MESH)
    for m in range(1, narrows):
        pl.semaphore_signal(barrier, inc=1, device_id={"wide": w, "narrow": narrow_at[m]}, device_id_type=MESH)

    sent = []

    def send(source, target, wide, narrow):
        at = len(sent)
        copy = pltpu.make_async_remote_copy(
            src_ref=source, dst_ref=target, send_sem=send_sem.at[at], recv_sem=recv_sem.at[at],
            device_id={"wide": wide, "narrow": narrow}, device_id_type=MESH,
        )
        copy.start()
        sent.append(copy)
        return copy

    def fetch(source, target, at):
        copy = pltpu.make_async_copy(source, target, local_sem.at[at])
        copy.start()
        return copy

    get_pairs = fetch(pairs_ref, pairs, 0)
    get_screen = fetch(screen_ref, screen, 1)
    get_trial = fetch(trial_ref, trial.at[n], 2)
    depth = virt.shape[2]
    get_virt = [
        fetch(virt_ref.at[:, pl.ds(pl.multiple_of(z_at[k] * depth, depth), depth)], virt.at[k], 3 + k)
        for k in range(zs)
    ]

    pl.semaphore_wait(barrier, wides + narrows - 2)

    def share(block, of):
        return trial.at[block, pl.ds(pl.multiple_of(of * cut, cut), cut)]

    mine = trial_ref.at[pl.ds(pl.multiple_of(w * cut, cut), cut)]
    along_z = {k: send(mine, share(n, w), w, z_at[k] * CORES + c) for k in range(1, zs)}
    to_mate = send(trial_ref, trial.at[n], w, z * CORES + mate)

    get_pairs.wait()
    get_screen.wait()
    product = lax.dot_general(
        screen[...], pairs[...], (((0,), (0,)), ((), ())), preferred_element_type=jnp.float32
    )
    aux = wides * narrows
    rows = tiles.shape[2]
    halves_j = orbitals // LANES
    own_i = rows // halves_j
    for i in range(own_i):
        for h in range(halves_j):
            t = i * halves_j + h
            staged[pl.ds(h * own_i + i, aux, stride=rows), :] = product[:, t * LANES : (t + 1) * LANES]
    tiles[...] = staged[...].reshape(tiles.shape).astype(jnp.bfloat16)
    tiles_wide[w] = tiles[w]
    tiles_in = [send(tiles.at[wide_at[m]], tiles_wide.at[w], wide_at[m], n) for m in wide_order]

    def chunk(k):
        first = z_at[k] * CORES
        wide_rows = jnp.concatenate([trial[first + p] for p in range(CORES)], axis=1)
        return lax.dot_general(
            wide_rows, virt[k], (((1,), (1,)), ((), ())), preferred_element_type=jnp.float32
        )

    get_trial.wait()
    get_virt[0].wait()
    to_mate.wait_recv()
    total[...] = chunk(0)

    across = {}
    for k in range(1, zs):
        along_z[k].wait_recv()
        block = z_at[k] * CORES + c
        across[k] = [send(share(block, w), share(block, w), wide_at[m], n) for m in wide_order]

    for copy in tiles_in:
        copy.wait_recv()
    tiles_all[n] = tiles_wide[:, n]
    tiles_done = [
        send(tiles_wide.at[:, narrow_at[m]], tiles_all.at[n], w, narrow_at[m]) for m in range(1, narrows)
    ]

    relayed = {}
    for k in range(1, zs):
        for copy in across[k]:
            copy.wait_recv()
        block = z_at[k] * CORES + c
        relayed[k] = send(trial.at[block], trial.at[block], w, z * CORES + mate)
    for k in range(1, zs - 1):
        get_virt[k].wait()
        relayed[k].wait_recv()
        total[...] += chunk(k)

    for copy in tiles_done:
        copy.wait_recv()
    columns = []
    for h in range(halves_j):
        parts = [
            tiles_all[b, a].astype(jnp.float32)[h * own_i : (h + 1) * own_i]
            for a in range(wides)
            for b in range(narrows)
        ]
        columns.append(jnp.concatenate(parts, axis=0))
    screened = jnp.concatenate(columns, axis=1).astype(jnp.bfloat16)

    get_virt[zs - 1].wait()
    relayed[zs - 1].wait_recv()
    whole = (total[...] + chunk(zs - 1)).astype(jnp.bfloat16)

    product = jnp.dot(screened, whole, preferred_element_type=jnp.float32)
    for b in range(narrows):
        to_core[b] = product[:, b * LANES : (b + 1) * LANES].astype(jnp.bfloat16)
    order = list(range(zs - 1, -1, -1))
    from_mate, from_wides, from_zs = {}, {}, {}
    for k in order:
        from_mate[k] = send(
            to_core.at[z_at[k] * CORES + mate], from_core.at[k], w, z * CORES + mate
        )
    for b in range(narrows):
        partial[b] = product[:, b * LANES : (b + 1) * LANES]
    early = len(sent)
    for k in order:
        from_mate[k].wait_recv()
        value = partial[z_at[k] * CORES + c] + from_core[k].astype(jnp.float32)
        summed[k] = value
        to_wide[k] = value.astype(jnp.bfloat16)
        from_wides[k] = [
            send(
                to_wide.at[k, pl.ds(pl.multiple_of(wide_at[m] * cut, cut), cut)],
                from_wide.at[k, m - 1], wide_at[m], n,
            )
            for m in wide_order
        ]
    for copy in sent[:early]:
        copy.wait_send()
    for k in order:
        value = summed[k, pl.ds(pl.multiple_of(w * cut, cut), cut), :]
        for copy in from_wides[k]:
            copy.wait_recv()
        for m in range(1, wides):
            value = value + from_wide[k, m - 1].astype(jnp.float32)
        if k:
            to_z[k - 1] = value.astype(jnp.bfloat16)
            from_zs[k] = send(to_z.at[k - 1], from_z.at[k - 1], w, z_at[k] * CORES + c)
    for copy in sent[early : early + zs * (wides - 1)]:
        copy.wait_send()
    for k in range(1, zs):
        from_zs[k].wait_recv()
        value = value + from_z[k - 1].astype(jnp.float32)
    out_ref[...] = value
    for copy in sent[early + zs * (wides - 1) :]:
        copy.wait_send()


def fused(wides, narrows, pair_integrals, screening, virtual_integrals, trials):
    zs = narrows // CORES
    orbitals, columns = trials.shape[1:]
    virtuals = virtual_integrals.shape[1]
    aux = screening.shape[1]
    pairs_here = pair_integrals.shape[0]
    rows = pairs_here // LANES
    cut = orbitals // wides
    bf, f4 = jnp.bfloat16, jnp.float32
    copies = (zs - 1) * 2 + 1 + (zs - 1) * (wides - 1) + (wides - 1) + (narrows - 1)
    copies += zs + zs * (wides - 1) + (zs - 1)
    anywhere = pl.BlockSpec(memory_space=pl.ANY)
    operands = (pair_integrals.T, screening, virtual_integrals[0], trials[0])
    out = pl.pallas_call(
        functools.partial(kernel, wides, narrows),
        out_shape=jax.ShapeDtypeStruct((cut, columns), f4),
        in_specs=[anywhere] * 4,
        out_specs=pl.BlockSpec(memory_space=pltpu.VMEM),
        scratch_shapes=[
            pltpu.VMEM((aux, pairs_here), bf),
            pltpu.VMEM(screening.shape, bf),
            pltpu.VMEM((zs, virtuals, virtuals // zs), bf),
            pltpu.VMEM((narrows, orbitals, columns), bf),
            pltpu.VMEM((aux * rows, LANES), f4),
            pltpu.VMEM((wides, narrows, rows, LANES), bf),
            pltpu.VMEM((wides, narrows, rows, LANES), bf),
            pltpu.VMEM((narrows, wides, rows, LANES), bf),
            pltpu.VMEM((orbitals, virtuals), f4),
            pltpu.VMEM((narrows, orbitals, columns), f4),
            pltpu.VMEM((narrows, orbitals, columns), bf),
            pltpu.VMEM((zs, orbitals, columns), bf),
            pltpu.VMEM((zs, orbitals, columns), f4),
            pltpu.VMEM((zs, orbitals, columns), bf),
            pltpu.VMEM((zs, wides - 1, cut, columns), bf),
            pltpu.VMEM((zs - 1, cut, columns), bf),
            pltpu.VMEM((zs - 1, cut, columns), bf),
            pltpu.SemaphoreType.DMA((3 + zs,)),
            pltpu.SemaphoreType.DMA((copies,)),
            pltpu.SemaphoreType.DMA((copies,)),
        ],
        compiler_params=pltpu.CompilerParams(
            collective_id=0, has_side_effects=True, vmem_limit_bytes=32 * 2**20
        ),
    )(*[pltpu.with_memory_space_constraint(x, pltpu.HBM) for x in operands])
    return out.T[:, None, :]


def plain(pair_integrals, screening, virtual_integrals, trials):
    orbitals = trials.shape[1]
    screened = jnp.dot(pair_integrals, screening, preferred_element_type=jnp.float32).astype(
        jnp.bfloat16
    )
    blocks = screened.reshape((1, 1) + screened.shape)
    owned_tiles = lax.all_to_all(
        lax.all_to_all(blocks, "wide", split_axis=3, concat_axis=0, tiled=True),
        "narrow",
        split_axis=3,
        concat_axis=1,
        tiled=True,
    )
    pair_tiles = owned_tiles.reshape(orbitals, orbitals, owned_tiles.shape[3])
    whole_trials = lax.all_gather(trials, "narrow", axis=2, tiled=True)
    halves = jnp.einsum(
        "qab,sjb->qasj", virtual_integrals, whole_trials, preferred_element_type=jnp.float32
    ).astype(jnp.bfloat16)
    shares = lax.psum_scatter(
        jnp.einsum("qasj,ijq->asi", halves, pair_tiles, preferred_element_type=jnp.float32),
        "narrow",
        scatter_dimension=0,
        tiled=True,
    )
    return lax.psum_scatter(shares, "wide", scatter_dimension=2, tiled=True)


def per_device(wides, narrows, pair_integrals, screening, virtual_integrals, trials):
    trial_count, orbitals, columns = trials.shape
    own_i = pair_integrals.shape[0] // orbitals
    fits = (
        trial_count == 1
        and virtual_integrals.shape[0] == 1
        and screening.shape[1] == wides * narrows
        and columns == LANES
        and orbitals % LANES == 0
        and orbitals % (16 * wides) == 0
        and narrows % CORES == 0
        and wides & (wides - 1) == 0
        and narrows & (narrows - 1) == 0
        and wides > 1
        and narrows > CORES
        and own_i % 8 == 0
        and (own_i * orbitals // LANES) % 16 == 0
    )
    if fits:
        return fused(wides, narrows, pair_integrals, screening, virtual_integrals, trials)
    return plain(pair_integrals, screening, virtual_integrals, trials)


def solution(mesh):
    return jax.shard_map(
        functools.partial(per_device, mesh.shape["wide"], mesh.shape["narrow"]),
        mesh=mesh,
        in_specs=(
            P(("wide", "narrow"), None),
            P(),
            P(("wide", "narrow"), None, None),
            P(None, None, "narrow"),
        ),
        out_specs=P("narrow", None, "wide"),
        check_vma=False,
    )
```

```python
import functools

import jax
import jax.numpy as jnp
from jax import lax
from jax.experimental import pallas as pl
from jax.experimental.pallas import tpu as pltpu
from jax.sharding import PartitionSpec as P

LANES = 128
CORES = 2
MESH = pl.DeviceIdType.MESH


def flipped(index, mask):
    bit = 1
    result = index
    while bit <= mask:
        if mask & bit:
            result = result + bit * (1 - 2 * lax.rem(lax.div(index, bit), 2))
        bit *= 2
    return result


def kernel(
    wides, narrows, pairs_ref, screen_ref, virt_ref, trial_ref, out_ref,
    pairs, screen, virt, trial, staged, tiles, tiles_wide, tiles_all, total, partial,
    to_core, from_core, summed, to_wide, from_wide, to_z, from_z,
    local_sem, send_sem, recv_sem,
):
    zs = narrows // CORES
    w, n = lax.axis_index("wide"), lax.axis_index("narrow")
    z, c = lax.div(n, CORES), lax.rem(n, CORES)
    mate = 1 - c
    orbitals = trial.shape[1]
    cut = orbitals // wides
    wide_at = [flipped(w, m) for m in range(wides)]
    z_at = [flipped(z, k) for k in range(zs)]
    narrow_at = [flipped(n, m) for m in range(narrows)]
    wide_order = [wides - 1] + list(range(1, wides - 1))

    barrier = pltpu.get_barrier_semaphore()
    for m in range(1, wides):
        pl.semaphore_signal(barrier, inc=1, device_id={"wide": wide_at[m], "narrow": n}, device_id_type=MESH)
    for m in range(1, narrows):
        pl.semaphore_signal(barrier, inc=1, device_id={"wide": w, "narrow": narrow_at[m]}, device_id_type=MESH)

    sent = []

    def send(source, target, wide, narrow):
        at = len(sent)
        copy = pltpu.make_async_remote_copy(
            src_ref=source, dst_ref=target, send_sem=send_sem.at[at], recv_sem=recv_sem.at[at],
            device_id={"wide": wide, "narrow": narrow}, device_id_type=MESH,
        )
        copy.start()
        sent.append(copy)
        return copy

    def fetch(source, target, at):
        copy = pltpu.make_async_copy(source, target, local_sem.at[at])
        copy.start()
        return copy

    get_trial = fetch(trial_ref, trial.at[n], 2)
    get_pairs = fetch(pairs_ref, pairs, 0)
    get_screen = fetch(screen_ref, screen, 1)

    pl.semaphore_wait(barrier, wides + narrows - 2)

    def share(block, of):
        return trial.at[block, pl.ds(pl.multiple_of(of * cut, cut), cut)]

    get_trial.wait()
    along_z = {k: send(share(n, w), share(n, w), w, z_at[k] * CORES + c) for k in range(1, zs)}
    to_mate = send(trial.at[n], trial.at[n], w, z * CORES + mate)
    depth = virt.shape[2]
    get_virt = [
        fetch(virt_ref.at[:, pl.ds(pl.multiple_of(z_at[k] * depth, depth), depth)], virt.at[k], 3 + k)
        for k in range(zs)
    ]

    get_pairs.wait()
    get_screen.wait()
    product = lax.dot_general(
        screen[...], pairs[...], (((0,), (0,)), ((), ())), preferred_element_type=jnp.float32
    )
    aux = wides * narrows
    rows = tiles.shape[2]
    halves_j = orbitals // LANES
    own_i = rows // halves_j
    for i in range(own_i):
        for h in range(halves_j):
            t = i * halves_j + h
            staged[pl.ds(h * own_i + i, aux, stride=rows), :] = product[:, t * LANES : (t + 1) * LANES]
    tiles[...] = staged[...].reshape(tiles.shape).astype(jnp.bfloat16)
    tiles_wide[w] = tiles[w]
    tiles_in = [send(tiles.at[wide_at[m]], tiles_wide.at[w], wide_at[m], n) for m in wide_order]

    def chunk(k):
        first = z_at[k] * CORES
        wide_rows = jnp.concatenate([trial[first + p] for p in range(CORES)], axis=1)
        return lax.dot_general(
            wide_rows, virt[k], (((1,), (1,)), ((), ())), preferred_element_type=jnp.float32
        )

    get_virt[0].wait()
    to_mate.wait_recv()
    total[...] = chunk(0)

    across = {}
    for k in range(1, zs):
        along_z[k].wait_recv()
        block = z_at[k] * CORES + c
        across[k] = [send(share(block, w), share(block, w), wide_at[m], n) for m in wide_order]

    for copy in tiles_in:
        copy.wait_recv()
    tiles_all[n] = tiles_wide[:, n]
    tiles_done = [
        send(tiles_wide.at[:, narrow_at[m]], tiles_all.at[n], w, narrow_at[m])
        for m in range(narrows - 1, 0, -1)
    ]

    relayed = {}
    for k in range(1, zs):
        for copy in across[k]:
            copy.wait_recv()
        block = z_at[k] * CORES + c
        relayed[k] = send(trial.at[block], trial.at[block], w, z * CORES + mate)
    for k in range(1, zs - 1):
        get_virt[k].wait()
        relayed[k].wait_recv()
        total[...] += chunk(k)

    get_virt[zs - 1].wait()
    relayed[zs - 1].wait_recv()
    for copy in tiles_done:
        copy.wait_recv()
    columns = []
    for h in range(halves_j):
        parts = [
            tiles_all[b, a].astype(jnp.float32)[h * own_i : (h + 1) * own_i]
            for a in range(wides)
            for b in range(narrows)
        ]
        columns.append(jnp.concatenate(parts, axis=0))
    screened = jnp.concatenate(columns, axis=1).astype(jnp.bfloat16)

    whole = (total[...] + chunk(zs - 1)).astype(jnp.bfloat16)

    product = jnp.dot(screened, whole, preferred_element_type=jnp.float32)
    for b in range(narrows):
        to_core[b] = product[:, b * LANES : (b + 1) * LANES].astype(jnp.bfloat16)
    order = list(range(zs - 1, -1, -1))
    from_mate, from_wides, from_zs = {}, {}, {}
    for k in order:
        from_mate[k] = send(
            to_core.at[z_at[k] * CORES + mate], from_core.at[k], w, z * CORES + mate
        )
    for b in range(narrows):
        partial[b] = product[:, b * LANES : (b + 1) * LANES]
    early = len(sent)
    for k in order:
        from_mate[k].wait_recv()
        value = partial[z_at[k] * CORES + c] + from_core[k].astype(jnp.float32)
        summed[k] = value
        to_wide[k] = value.astype(jnp.bfloat16)
        from_wides[k] = [
            send(
                to_wide.at[k, pl.ds(pl.multiple_of(wide_at[m] * cut, cut), cut)],
                from_wide.at[k, m - 1], wide_at[m], n,
            )
            for m in wide_order
        ]
    for copy in sent[:early]:
        copy.wait_send()
    for k in order:
        value = summed[k, pl.ds(pl.multiple_of(w * cut, cut), cut), :]
        for copy in from_wides[k]:
            copy.wait_recv()
        for m in range(1, wides):
            value = value + from_wide[k, m - 1].astype(jnp.float32)
        if k:
            to_z[k - 1] = value.astype(jnp.bfloat16)
            from_zs[k] = send(to_z.at[k - 1], from_z.at[k - 1], w, z_at[k] * CORES + c)
    for copy in sent[early : early + zs * (wides - 1)]:
        copy.wait_send()
    for k in range(1, zs):
        from_zs[k].wait_recv()
        value = value + from_z[k - 1].astype(jnp.float32)
    out_ref[...] = value
    for copy in sent[early + zs * (wides - 1) :]:
        copy.wait_send()


def fused(wides, narrows, pair_integrals, screening, virtual_integrals, trials):
    zs = narrows // CORES
    orbitals, columns = trials.shape[1:]
    virtuals = virtual_integrals.shape[1]
    aux = screening.shape[1]
    pairs_here = pair_integrals.shape[0]
    rows = pairs_here // LANES
    cut = orbitals // wides
    bf, f4 = jnp.bfloat16, jnp.float32
    copies = (zs - 1) * 2 + 1 + (zs - 1) * (wides - 1) + (wides - 1) + (narrows - 1)
    copies += zs + zs * (wides - 1) + (zs - 1)
    anywhere = pl.BlockSpec(memory_space=pl.ANY)
    operands = (pair_integrals.T, screening, virtual_integrals[0], trials[0])
    out = pl.pallas_call(
        functools.partial(kernel, wides, narrows),
        out_shape=jax.ShapeDtypeStruct((cut, columns), f4),
        in_specs=[anywhere] * 4,
        out_specs=pl.BlockSpec(memory_space=pltpu.VMEM),
        scratch_shapes=[
            pltpu.VMEM((aux, pairs_here), bf),
            pltpu.VMEM(screening.shape, bf),
            pltpu.VMEM((zs, virtuals, virtuals // zs), bf),
            pltpu.VMEM((narrows, orbitals, columns), bf),
            pltpu.VMEM((aux * rows, LANES), f4),
            pltpu.VMEM((wides, narrows, rows, LANES), bf),
            pltpu.VMEM((wides, narrows, rows, LANES), bf),
            pltpu.VMEM((narrows, wides, rows, LANES), bf),
            pltpu.VMEM((orbitals, virtuals), f4),
            pltpu.VMEM((narrows, orbitals, columns), f4),
            pltpu.VMEM((narrows, orbitals, columns), bf),
            pltpu.VMEM((zs, orbitals, columns), bf),
            pltpu.VMEM((zs, orbitals, columns), f4),
            pltpu.VMEM((zs, orbitals, columns), bf),
            pltpu.VMEM((zs, wides - 1, cut, columns), bf),
            pltpu.VMEM((zs - 1, cut, columns), bf),
            pltpu.VMEM((zs - 1, cut, columns), bf),
            pltpu.SemaphoreType.DMA((3 + zs,)),
            pltpu.SemaphoreType.DMA((copies,)),
            pltpu.SemaphoreType.DMA((copies,)),
        ],
        compiler_params=pltpu.CompilerParams(
            collective_id=0, has_side_effects=True, vmem_limit_bytes=32 * 2**20
        ),
    )(*[pltpu.with_memory_space_constraint(x, pltpu.HBM) for x in operands])
    return out.T[:, None, :]


def plain(pair_integrals, screening, virtual_integrals, trials):
    orbitals = trials.shape[1]
    screened = jnp.dot(pair_integrals, screening, preferred_element_type=jnp.float32).astype(
        jnp.bfloat16
    )
    blocks = screened.reshape((1, 1) + screened.shape)
    owned_tiles = lax.all_to_all(
        lax.all_to_all(blocks, "wide", split_axis=3, concat_axis=0, tiled=True),
        "narrow",
        split_axis=3,
        concat_axis=1,
        tiled=True,
    )
    pair_tiles = owned_tiles.reshape(orbitals, orbitals, owned_tiles.shape[3])
    whole_trials = lax.all_gather(trials, "narrow", axis=2, tiled=True)
    halves = jnp.einsum(
        "qab,sjb->qasj", virtual_integrals, whole_trials, preferred_element_type=jnp.float32
    ).astype(jnp.bfloat16)
    shares = lax.psum_scatter(
        jnp.einsum("qasj,ijq->asi", halves, pair_tiles, preferred_element_type=jnp.float32),
        "narrow",
        scatter_dimension=0,
        tiled=True,
    )
    return lax.psum_scatter(shares, "wide", scatter_dimension=2, tiled=True)


def per_device(wides, narrows, pair_integrals, screening, virtual_integrals, trials):
    trial_count, orbitals, columns = trials.shape
    own_i = pair_integrals.shape[0] // orbitals
    fits = (
        trial_count == 1
        and virtual_integrals.shape[0] == 1
        and screening.shape[1] == wides * narrows
        and columns == LANES
        and orbitals % LANES == 0
        and orbitals % (16 * wides) == 0
        and narrows % CORES == 0
        and wides & (wides - 1) == 0
        and narrows & (narrows - 1) == 0
        and wides > 1
        and narrows > CORES
        and own_i % 8 == 0
        and (own_i * orbitals // LANES) % 16 == 0
    )
    if fits:
        return fused(wides, narrows, pair_integrals, screening, virtual_integrals, trials)
    return plain(pair_integrals, screening, virtual_integrals, trials)


def solution(mesh):
    return jax.shard_map(
        functools.partial(per_device, mesh.shape["wide"], mesh.shape["narrow"]),
        mesh=mesh,
        in_specs=(
            P(("wide", "narrow"), None),
            P(),
            P(("wide", "narrow"), None, None),
            P(None, None, "narrow"),
        ),
        out_specs=P("narrow", None, "wide"),
        check_vma=False,
    )
```

```python
import functools

import jax
import jax.numpy as jnp
from jax import lax
from jax.experimental import pallas as pl
from jax.experimental.pallas import tpu as pltpu
from jax.sharding import PartitionSpec as P

LANES = 128
CORES = 2
MESH = pl.DeviceIdType.MESH


def flipped(index, mask):
    bit = 1
    result = index
    while bit <= mask:
        if mask & bit:
            result = result + bit * (1 - 2 * lax.rem(lax.div(index, bit), 2))
        bit *= 2
    return result


def kernel(
    wides, narrows, pairs_ref, screen_ref, virt_ref, trial_ref, out_ref,
    pairs, screen, virt, trial, staged, tiles, tiles_all, total,
    summed, to_wide, from_wide, to_z, from_z,
    local_sem, send_sem, recv_sem,
):
    zs = narrows // CORES
    w, n = lax.axis_index("wide"), lax.axis_index("narrow")
    z, c = lax.div(n, CORES), lax.rem(n, CORES)
    mate = 1 - c
    orbitals = trial.shape[1]
    cut = orbitals // wides
    wide_at = [flipped(w, m) for m in range(wides)]
    z_at = [flipped(z, k) for k in range(zs)]
    wide_order = [wides - 1] + list(range(1, wides - 1))
    order = list(range(zs - 1, -1, -1))
    peers = [(m, k) for k in order for m in wide_order + [0] if m or k]

    barrier = pltpu.get_barrier_semaphore()
    for m, k in peers:
        peer = {"wide": wide_at[m], "narrow": z_at[k] * CORES + c}
        pl.semaphore_signal(barrier, inc=1, device_id=peer, device_id_type=MESH)
    pl.semaphore_signal(
        barrier, inc=1, device_id={"wide": w, "narrow": z * CORES + mate}, device_id_type=MESH
    )

    sent = []

    def send(source, target, wide, narrow):
        at = len(sent)
        copy = pltpu.make_async_remote_copy(
            src_ref=source, dst_ref=target, send_sem=send_sem.at[at], recv_sem=recv_sem.at[at],
            device_id={"wide": wide, "narrow": narrow}, device_id_type=MESH,
        )
        copy.start()
        sent.append(copy)
        return copy

    def to_mate(source, target):
        return send(source, target, w, z * CORES + mate)

    def fetch(source, target, at):
        copy = pltpu.make_async_copy(source, target, local_sem.at[at])
        copy.start()
        return copy

    get_trial = fetch(trial_ref, trial.at[n], 2)
    get_pairs = fetch(pairs_ref, pairs, 0)
    get_screen = fetch(screen_ref, screen, 1)

    pl.semaphore_wait(barrier, len(peers) + 1)

    def share(block, of):
        return trial.at[block, pl.ds(pl.multiple_of(of * cut, cut), cut)]

    get_trial.wait()
    along_z = {k: send(share(n, w), share(n, w), w, z_at[k] * CORES + c) for k in range(1, zs)}
    own_block = to_mate(trial.at[n], trial.at[n])

    depth = virt.shape[4]

    def rows_for(core, k):
        return virt_ref.at[:, core, :, pl.ds(pl.multiple_of(z_at[k] * depth, depth), depth)]

    get_virt = [fetch(rows_for(c, k), virt.at[k, c], 3 + k) for k in range(zs)]
    mate_virt = [to_mate(rows_for(mate, k), virt.at[k, c]) for k in range(zs)]

    get_pairs.wait()
    get_screen.wait()
    product = lax.dot_general(
        screen[...], pairs[...], (((0,), (0,)), ((), ())), preferred_element_type=jnp.float32
    )
    aux = wides * narrows
    rows = tiles.shape[2]
    halves_j = orbitals // LANES
    own_i = rows // halves_j
    for i in range(own_i):
        for h in range(halves_j):
            t = i * halves_j + h
            staged[pl.ds(h * own_i + i, aux, stride=rows), :] = product[:, t * LANES : (t + 1) * LANES]
    tiles[...] = staged[...].reshape(tiles.shape).astype(jnp.bfloat16)
    tiles_in = {k: [] for k in order}
    for m, k in peers:
        source = tiles.at[wide_at[m], pl.ds(z_at[k] * CORES, CORES)]
        tiles_in[k].append(send(source, tiles_all.at[c, w, z], wide_at[m], z_at[k] * CORES + c))
    tiles_all[c, w, z] = tiles[w, pl.ds(z * CORES, CORES)]

    def chunk(k):
        first = z_at[k] * CORES
        wide_rows = jnp.concatenate([trial[first + p] for p in range(CORES)], axis=1)
        return lax.dot_general(
            wide_rows, virt[k].reshape(-1, depth), (((1,), (1,)), ((), ())),
            preferred_element_type=jnp.float32,
        )

    across = {}
    for k in range(1, zs):
        along_z[k].wait_recv()
        block = z_at[k] * CORES + c
        across[k] = [send(share(block, w), share(block, w), wide_at[m], n) for m in wide_order]

    get_virt[0].wait()
    own_block.wait_recv()
    mate_virt[0].wait_recv()
    total[...] = chunk(0)

    relayed, tiles_done = {}, []

    def relay_tiles(k):
        for copy in tiles_in[k]:
            copy.wait_recv()
        group = tiles_all.at[c, :, z_at[k]]
        tiles_done.append(to_mate(group, group))

    for k in range(1, zs):
        relay_tiles(zs - k)
        for copy in across[k]:
            copy.wait_recv()
        block = z_at[k] * CORES + c
        relayed[k] = to_mate(trial.at[block], trial.at[block])
    relay_tiles(0)
    for k in range(1, zs):
        get_virt[k].wait()
        mate_virt[k].wait_recv()
        relayed[k].wait_recv()
        if k < zs - 1:
            total[...] += chunk(k)
    for copy in tiles_done:
        copy.wait_recv()

    def screened(q):
        columns = []
        for h in range(halves_j):
            parts = [
                tiles_all[p, a, b, q].astype(jnp.float32)[h * own_i : (h + 1) * own_i]
                for a in range(wides)
                for b in range(zs)
                for p in range(CORES)
            ]
            columns.append(jnp.concatenate(parts, axis=0))
        return jnp.concatenate(columns, axis=1).astype(jnp.bfloat16)

    whole = (total[...] + chunk(zs - 1)).astype(jnp.bfloat16)

    span = zs * LANES
    product = sum(
        jnp.dot(screened(q), whole[:, q * span : (q + 1) * span], preferred_element_type=jnp.float32)
        for q in range(CORES)
    )
    for b in range(zs):
        to_wide[b] = product[:, b * LANES : (b + 1) * LANES].astype(jnp.bfloat16)
    from_wides, from_zs = {}, {}
    early = len(sent)
    for k in order:
        from_wides[k] = [
            send(
                to_wide.at[z_at[k], pl.ds(pl.multiple_of(wide_at[m] * cut, cut), cut)],
                from_wide.at[k, m - 1], wide_at[m], n,
            )
            for m in wide_order
        ]
    for b in range(zs):
        summed[b] = product[:, b * LANES : (b + 1) * LANES]
    for copy in sent[:early]:
        copy.wait_send()
    for k in order:
        value = summed[z_at[k], pl.ds(pl.multiple_of(w * cut, cut), cut), :]
        for copy in from_wides[k]:
            copy.wait_recv()
        for m in range(1, wides):
            value = value + from_wide[k, m - 1].astype(jnp.float32)
        if k:
            to_z[k - 1] = value.astype(jnp.bfloat16)
            from_zs[k] = send(to_z.at[k - 1], from_z.at[k - 1], w, z_at[k] * CORES + c)
    for copy in sent[early : early + zs * (wides - 1)]:
        copy.wait_send()
    for k in range(1, zs):
        from_zs[k].wait_recv()
        value = value + from_z[k - 1].astype(jnp.float32)
    out_ref[...] = value
    for copy in sent[early + zs * (wides - 1) :]:
        copy.wait_send()


def fused(wides, narrows, pair_integrals, screening, virtual_integrals, trials):
    zs = narrows // CORES
    orbitals, columns = trials.shape[1:]
    virtuals = virtual_integrals.shape[1]
    aux = screening.shape[1]
    pairs_here = pair_integrals.shape[0]
    rows = pairs_here // LANES
    cut = orbitals // wides
    bf, f4 = jnp.bfloat16, jnp.float32
    copies = (zs - 1) * 2 + 1 + zs + (wides * zs - 1) + (zs - 1) * (wides - 1) + zs
    copies += zs * (wides - 1) + (zs - 1)
    anywhere = pl.BlockSpec(memory_space=pl.ANY)
    slabs = virtual_integrals.reshape(zs, CORES, columns, virtuals)
    operands = (pair_integrals.T, screening, slabs, trials[0])
    out = pl.pallas_call(
        functools.partial(kernel, wides, narrows),
        out_shape=jax.ShapeDtypeStruct((cut, columns), f4),
        in_specs=[anywhere] * 4,
        out_specs=pl.BlockSpec(memory_space=pltpu.VMEM),
        scratch_shapes=[
            pltpu.VMEM((aux, pairs_here), bf),
            pltpu.VMEM(screening.shape, bf),
            pltpu.VMEM((zs, CORES, zs, columns, virtuals // zs), bf),
            pltpu.VMEM((narrows, orbitals, columns), bf),
            pltpu.VMEM((aux * rows, LANES), f4),
            pltpu.VMEM((wides, narrows, rows, LANES), bf),
            pltpu.VMEM((CORES, wides, zs, CORES, rows, LANES), bf),
            pltpu.VMEM((orbitals, virtuals), f4),
            pltpu.VMEM((zs, orbitals, columns), f4),
            pltpu.VMEM((zs, orbitals, columns), bf),
            pltpu.VMEM((zs, wides - 1, cut, columns), bf),
            pltpu.VMEM((zs - 1, cut, columns), bf),
            pltpu.VMEM((zs - 1, cut, columns), bf),
            pltpu.SemaphoreType.DMA((3 + zs,)),
            pltpu.SemaphoreType.DMA((copies,)),
            pltpu.SemaphoreType.DMA((copies,)),
        ],
        compiler_params=pltpu.CompilerParams(
            collective_id=0, has_side_effects=True, vmem_limit_bytes=32 * 2**20
        ),
    )(*[pltpu.with_memory_space_constraint(x, pltpu.HBM) for x in operands])
    return out.T[:, None, :]


def plain(pair_integrals, screening, virtual_integrals, trials):
    orbitals = trials.shape[1]
    screened = jnp.dot(pair_integrals, screening, preferred_element_type=jnp.float32).astype(
        jnp.bfloat16
    )
    blocks = screened.reshape((1, 1) + screened.shape)
    owned_tiles = lax.all_to_all(
        lax.all_to_all(blocks, "wide", split_axis=3, concat_axis=0, tiled=True),
        "narrow",
        split_axis=3,
        concat_axis=1,
        tiled=True,
    )
    pair_tiles = owned_tiles.reshape(orbitals, orbitals, owned_tiles.shape[3])
    whole_trials = lax.all_gather(trials, "narrow", axis=2, tiled=True)
    halves = jnp.einsum(
        "qab,sjb->qasj", virtual_integrals, whole_trials, preferred_element_type=jnp.float32
    ).astype(jnp.bfloat16)
    shares = lax.psum_scatter(
        jnp.einsum("qasj,ijq->asi", halves, pair_tiles, preferred_element_type=jnp.float32),
        "narrow",
        scatter_dimension=0,
        tiled=True,
    )
    return lax.psum_scatter(shares, "wide", scatter_dimension=2, tiled=True)


def per_device(wides, narrows, pair_integrals, screening, virtual_integrals, trials):
    trial_count, orbitals, columns = trials.shape
    own_i = pair_integrals.shape[0] // orbitals
    fits = (
        trial_count == 1
        and virtual_integrals.shape[0] == 1
        and screening.shape[1] == wides * narrows
        and columns == LANES
        and orbitals % LANES == 0
        and orbitals % (16 * wides) == 0
        and narrows % CORES == 0
        and wides & (wides - 1) == 0
        and narrows & (narrows - 1) == 0
        and wides > 1
        and narrows > CORES
        and own_i % 8 == 0
        and (own_i * orbitals // LANES) % 16 == 0
    )
    if fits:
        return fused(wides, narrows, pair_integrals, screening, virtual_integrals, trials)
    return plain(pair_integrals, screening, virtual_integrals, trials)


def solution(mesh):
    return jax.shard_map(
        functools.partial(per_device, mesh.shape["wide"], mesh.shape["narrow"]),
        mesh=mesh,
        in_specs=(
            P(("wide", "narrow"), None),
            P(),
            P(("wide", "narrow"), None, None),
            P(None, None, "narrow"),
        ),
        out_specs=P("narrow", None, "wide"),
        check_vma=False,
    )
```

```python
import functools

import jax
import jax.numpy as jnp
from jax import lax
from jax.experimental import pallas as pl
from jax.experimental.pallas import tpu as pltpu
from jax.sharding import PartitionSpec as P

LANES = 128
CORES = 2
MESH = pl.DeviceIdType.MESH


def flipped(index, mask):
    bit = 1
    result = index
    while bit <= mask:
        if mask & bit:
            result = result + bit * (1 - 2 * lax.rem(lax.div(index, bit), 2))
        bit *= 2
    return result


def kernel(
    wides, narrows, pairs_ref, screen_ref, virt_ref, trial_ref, out_ref,
    pairs, screen, virt, trial, staged, tiles, tiles_all, screened, total,
    summed, to_wide, from_wide, to_z, from_z,
    local_sem, send_sem, recv_sem,
):
    zs = narrows // CORES
    w, n = lax.axis_index("wide"), lax.axis_index("narrow")
    z, c = lax.div(n, CORES), lax.rem(n, CORES)
    mate = 1 - c
    orbitals = trial.shape[1]
    cut = orbitals // wides
    wide_at = [flipped(w, m) for m in range(wides)]
    z_at = [flipped(z, k) for k in range(zs)]
    wide_order = [wides - 1] + list(range(1, wides - 1))
    order = list(range(zs - 1, -1, -1))
    peers = [(m, k) for k in order for m in wide_order + [0] if m or k]

    barrier = pltpu.get_barrier_semaphore()
    for m, k in peers:
        peer = {"wide": wide_at[m], "narrow": z_at[k] * CORES + c}
        pl.semaphore_signal(barrier, inc=1, device_id=peer, device_id_type=MESH)
    pl.semaphore_signal(
        barrier, inc=1, device_id={"wide": w, "narrow": z * CORES + mate}, device_id_type=MESH
    )

    sent = []

    def send(source, target, wide, narrow):
        at = len(sent)
        copy = pltpu.make_async_remote_copy(
            src_ref=source, dst_ref=target, send_sem=send_sem.at[at], recv_sem=recv_sem.at[at],
            device_id={"wide": wide, "narrow": narrow}, device_id_type=MESH,
        )
        copy.start()
        sent.append(copy)
        return copy

    def to_mate(source, target):
        return send(source, target, w, z * CORES + mate)

    def fetch(source, target, at):
        copy = pltpu.make_async_copy(source, target, local_sem.at[at])
        copy.start()
        return copy

    get_trial = fetch(trial_ref, trial.at[n], 2)
    get_pairs = fetch(pairs_ref, pairs, 0)
    get_screen = fetch(screen_ref, screen, 1)

    pl.semaphore_wait(barrier, len(peers) + 1)

    def share(block, of):
        return trial.at[block, pl.ds(pl.multiple_of(of * cut, cut), cut)]

    get_trial.wait()
    along_z = {k: send(share(n, w), share(n, w), w, z_at[k] * CORES + c) for k in range(1, zs)}
    own_block = to_mate(trial.at[n], trial.at[n])

    depth = virt.shape[4]

    def rows_for(core, k):
        return virt_ref.at[:, core, :, pl.ds(pl.multiple_of(z_at[k] * depth, depth), depth)]

    get_virt = [fetch(rows_for(c, k), virt.at[k, c], 3 + k) for k in range(zs)]
    mate_virt = [to_mate(rows_for(mate, k), virt.at[k, c]) for k in range(zs)]

    get_pairs.wait()
    get_screen.wait()
    product = lax.dot_general(
        screen[...], pairs[...], (((0,), (0,)), ((), ())), preferred_element_type=jnp.float32
    )
    aux = wides * narrows
    rows = tiles.shape[2]
    halves_j = orbitals // LANES
    own_i = rows // halves_j
    for i in range(own_i):
        for h in range(halves_j):
            t = i * halves_j + h
            staged[pl.ds(h * own_i + i, aux, stride=rows), :] = product[:, t * LANES : (t + 1) * LANES]
    tiles[...] = staged[...].reshape(tiles.shape).astype(jnp.bfloat16)
    tiles_in = {k: [] for k in order}
    for m, k in peers:
        source = tiles.at[wide_at[m], pl.ds(z_at[k] * CORES, CORES)]
        tiles_in[k].append(send(source, tiles_all.at[c, w, z], wide_at[m], z_at[k] * CORES + c))
    tiles_all[c, w, z] = tiles[w, pl.ds(z * CORES, CORES)]

    def chunk(k):
        first = z_at[k] * CORES
        wide_rows = jnp.concatenate([trial[first + p] for p in range(CORES)], axis=1)
        return lax.dot_general(
            wide_rows, virt[k].reshape(-1, depth), (((1,), (1,)), ((), ())),
            preferred_element_type=jnp.float32,
        )

    across = {}
    for k in range(1, zs):
        along_z[k].wait_recv()
        block = z_at[k] * CORES + c
        across[k] = [send(share(block, w), share(block, w), wide_at[m], n) for m in wide_order]

    get_virt[0].wait()
    own_block.wait_recv()
    mate_virt[0].wait_recv()
    total[...] = chunk(0)

    relayed, tiles_done = {}, {}

    def relay_tiles(k):
        for copy in tiles_in[k]:
            copy.wait_recv()
        group = tiles_all.at[c, :, z_at[k]]
        tiles_done[k] = to_mate(group, group)

    def assemble(k):
        tall = CORES * own_i
        for a in range(wides):
            at = pl.ds(pl.multiple_of((a * zs + z_at[k]) * tall, tall), tall)
            for q in range(CORES):
                parts = [tiles_all[p, a, z_at[k], q].astype(jnp.float32) for p in range(CORES)]
                for h in range(halves_j):
                    both = jnp.concatenate([part[h * own_i : (h + 1) * own_i] for part in parts], axis=0)
                    screened[q, at, h * LANES : (h + 1) * LANES] = both.astype(jnp.bfloat16)

    def arrive(k):
        get_virt[k].wait()
        mate_virt[k].wait_recv()
        relayed[k].wait_recv()

    for k in range(1, zs):
        relay_tiles(zs - k)
        for copy in across[k]:
            copy.wait_recv()
        block = z_at[k] * CORES + c
        relayed[k] = to_mate(trial.at[block], trial.at[block])
        if k == zs - 1:
            relay_tiles(0)
        if k > 1:
            arrive(k - 1)
            tiles_done[zs - k + 1].wait_recv()
            total[...] += chunk(k - 1)
            assemble(zs - k + 1)
    tiles_done[1].wait_recv()
    assemble(1)
    tiles_done[0].wait_recv()
    arrive(zs - 1)
    assemble(0)
    whole = (total[...] + chunk(zs - 1)).astype(jnp.bfloat16)

    span = zs * LANES
    product = sum(
        jnp.dot(screened[q], whole[:, q * span : (q + 1) * span], preferred_element_type=jnp.float32)
        for q in range(CORES)
    )
    for b in range(zs):
        to_wide[b] = product[:, b * LANES : (b + 1) * LANES].astype(jnp.bfloat16)
    from_wides, from_zs = {}, {}
    early = len(sent)
    for k in order:
        from_wides[k] = [
            send(
                to_wide.at[z_at[k], pl.ds(pl.multiple_of(wide_at[m] * cut, cut), cut)],
                from_wide.at[k, m - 1], wide_at[m], n,
            )
            for m in wide_order
        ]
    for b in range(zs):
        summed[b] = product[:, b * LANES : (b + 1) * LANES]
    for copy in sent[:early]:
        copy.wait_send()
    for k in order:
        value = summed[z_at[k], pl.ds(pl.multiple_of(w * cut, cut), cut), :]
        for copy in from_wides[k]:
            copy.wait_recv()
        for m in range(1, wides):
            value = value + from_wide[k, m - 1].astype(jnp.float32)
        if k:
            to_z[k - 1] = value.astype(jnp.bfloat16)
            from_zs[k] = send(to_z.at[k - 1], from_z.at[k - 1], w, z_at[k] * CORES + c)
    for copy in sent[early : early + zs * (wides - 1)]:
        copy.wait_send()
    for k in range(1, zs):
        from_zs[k].wait_recv()
        value = value + from_z[k - 1].astype(jnp.float32)
    out_ref[...] = value
    for copy in sent[early + zs * (wides - 1) :]:
        copy.wait_send()


def fused(wides, narrows, pair_integrals, screening, virtual_integrals, trials):
    zs = narrows // CORES
    orbitals, columns = trials.shape[1:]
    virtuals = virtual_integrals.shape[1]
    aux = screening.shape[1]
    pairs_here = pair_integrals.shape[0]
    rows = pairs_here // LANES
    cut = orbitals // wides
    bf, f4 = jnp.bfloat16, jnp.float32
    copies = (zs - 1) * 2 + 1 + zs + (wides * zs - 1) + (zs - 1) * (wides - 1) + zs
    copies += zs * (wides - 1) + (zs - 1)
    anywhere = pl.BlockSpec(memory_space=pl.ANY)
    slabs = virtual_integrals.reshape(zs, CORES, columns, virtuals)
    operands = (pair_integrals.T, screening, slabs, trials[0])
    out = pl.pallas_call(
        functools.partial(kernel, wides, narrows),
        out_shape=jax.ShapeDtypeStruct((cut, columns), f4),
        in_specs=[anywhere] * 4,
        out_specs=pl.BlockSpec(memory_space=pltpu.VMEM),
        scratch_shapes=[
            pltpu.VMEM((aux, pairs_here), bf),
            pltpu.VMEM(screening.shape, bf),
            pltpu.VMEM((zs, CORES, zs, columns, virtuals // zs), bf),
            pltpu.VMEM((narrows, orbitals, columns), bf),
            pltpu.VMEM((aux * rows, LANES), f4),
            pltpu.VMEM((wides, narrows, rows, LANES), bf),
            pltpu.VMEM((CORES, wides, zs, CORES, rows, LANES), bf),
            pltpu.VMEM((CORES, orbitals, orbitals), bf),
            pltpu.VMEM((orbitals, virtuals), f4),
            pltpu.VMEM((zs, orbitals, columns), f4),
            pltpu.VMEM((zs, orbitals, columns), bf),
            pltpu.VMEM((zs, wides - 1, cut, columns), bf),
            pltpu.VMEM((zs - 1, cut, columns), bf),
            pltpu.VMEM((zs - 1, cut, columns), bf),
            pltpu.SemaphoreType.DMA((3 + zs,)),
            pltpu.SemaphoreType.DMA((copies,)),
            pltpu.SemaphoreType.DMA((copies,)),
        ],
        compiler_params=pltpu.CompilerParams(
            collective_id=0, has_side_effects=True, vmem_limit_bytes=32 * 2**20
        ),
    )(*[pltpu.with_memory_space_constraint(x, pltpu.HBM) for x in operands])
    return out.T[:, None, :]


def plain(pair_integrals, screening, virtual_integrals, trials):
    orbitals = trials.shape[1]
    screened = jnp.dot(pair_integrals, screening, preferred_element_type=jnp.float32).astype(
        jnp.bfloat16
    )
    blocks = screened.reshape((1, 1) + screened.shape)
    owned_tiles = lax.all_to_all(
        lax.all_to_all(blocks, "wide", split_axis=3, concat_axis=0, tiled=True),
        "narrow",
        split_axis=3,
        concat_axis=1,
        tiled=True,
    )
    pair_tiles = owned_tiles.reshape(orbitals, orbitals, owned_tiles.shape[3])
    whole_trials = lax.all_gather(trials, "narrow", axis=2, tiled=True)
    halves = jnp.einsum(
        "qab,sjb->qasj", virtual_integrals, whole_trials, preferred_element_type=jnp.float32
    ).astype(jnp.bfloat16)
    shares = lax.psum_scatter(
        jnp.einsum("qasj,ijq->asi", halves, pair_tiles, preferred_element_type=jnp.float32),
        "narrow",
        scatter_dimension=0,
        tiled=True,
    )
    return lax.psum_scatter(shares, "wide", scatter_dimension=2, tiled=True)


def per_device(wides, narrows, pair_integrals, screening, virtual_integrals, trials):
    trial_count, orbitals, columns = trials.shape
    own_i = pair_integrals.shape[0] // orbitals
    fits = (
        trial_count == 1
        and virtual_integrals.shape[0] == 1
        and screening.shape[1] == wides * narrows
        and columns == LANES
        and orbitals % LANES == 0
        and orbitals % (16 * wides) == 0
        and narrows % CORES == 0
        and wides & (wides - 1) == 0
        and narrows & (narrows - 1) == 0
        and wides > 1
        and narrows > CORES
        and own_i % 8 == 0
        and (own_i * orbitals // LANES) % 16 == 0
    )
    if fits:
        return fused(wides, narrows, pair_integrals, screening, virtual_integrals, trials)
    return plain(pair_integrals, screening, virtual_integrals, trials)


def solution(mesh):
    return jax.shard_map(
        functools.partial(per_device, mesh.shape["wide"], mesh.shape["narrow"]),
        mesh=mesh,
        in_specs=(
            P(("wide", "narrow"), None),
            P(),
            P(("wide", "narrow"), None, None),
            P(None, None, "narrow"),
        ),
        out_specs=P("narrow", None, "wide"),
        check_vma=False,
    )
```

```python
import functools

import jax
import jax.numpy as jnp
from jax import lax
from jax.experimental import pallas as pl
from jax.experimental.pallas import tpu as pltpu
from jax.sharding import PartitionSpec as P

LANES = 128
CORES = 2
MESH = pl.DeviceIdType.MESH


def flipped(index, mask):
    bit = 1
    result = index
    while bit <= mask:
        if mask & bit:
            result = result + bit * (1 - 2 * lax.rem(lax.div(index, bit), 2))
        bit *= 2
    return result


def kernel(
    wides, narrows, pairs_ref, screen_ref, virt_ref, trial_ref, out_ref,
    pairs, screen, virt, trial, staged, tiles, tiles_all, total, partial,
    to_core, from_core, summed, to_wide, from_wide, to_z, from_z,
    local_sem, send_sem, recv_sem,
):
    zs = narrows // CORES
    w, n = lax.axis_index("wide"), lax.axis_index("narrow")
    z, c = lax.div(n, CORES), lax.rem(n, CORES)
    mate = 1 - c
    orbitals = trial.shape[1]
    cut = orbitals // wides
    wide_at = [flipped(w, m) for m in range(wides)]
    z_at = [flipped(z, k) for k in range(zs)]
    narrow_at = [flipped(n, m) for m in range(narrows)]
    wide_order = [wides - 1] + list(range(1, wides - 1))

    barrier = pltpu.get_barrier_semaphore()
    peers = [(m, k) for k in range(narrows - 1, -1, -1) for m in wide_order + [0] if m or k]
    for m, k in peers:
        peer = {"wide": wide_at[m], "narrow": narrow_at[k]}
        pl.semaphore_signal(barrier, inc=1, device_id=peer, device_id_type=MESH)

    sent = []

    def send(source, target, wide, narrow):
        at = len(sent)
        copy = pltpu.make_async_remote_copy(
            src_ref=source, dst_ref=target, send_sem=send_sem.at[at], recv_sem=recv_sem.at[at],
            device_id={"wide": wide, "narrow": narrow}, device_id_type=MESH,
        )
        copy.start()
        sent.append(copy)
        return copy

    def fetch(source, target, at):
        copy = pltpu.make_async_copy(source, target, local_sem.at[at])
        copy.start()
        return copy

    get_trial = fetch(trial_ref, trial.at[n], 2)
    get_pairs = fetch(pairs_ref, pairs, 0)
    get_screen = fetch(screen_ref, screen, 1)

    pl.semaphore_wait(barrier, len(peers))

    def share(block, of):
        return trial.at[block, pl.ds(pl.multiple_of(of * cut, cut), cut)]

    get_trial.wait()
    along_z = {k: send(share(n, w), share(n, w), w, z_at[k] * CORES + c) for k in range(1, zs)}
    to_mate = send(trial.at[n], trial.at[n], w, z * CORES + mate)
    depth = virt.shape[2]
    get_virt = [
        fetch(virt_ref.at[:, pl.ds(pl.multiple_of(z_at[k] * depth, depth), depth)], virt.at[k], 3 + k)
        for k in range(zs)
    ]

    get_pairs.wait()
    get_screen.wait()
    product = lax.dot_general(
        screen[...], pairs[...], (((0,), (0,)), ((), ())), preferred_element_type=jnp.float32
    )
    aux = wides * narrows
    rows = tiles.shape[2]
    halves_j = orbitals // LANES
    own_i = rows // halves_j
    for i in range(own_i):
        for h in range(halves_j):
            t = i * halves_j + h
            staged[pl.ds(h * own_i + i, aux, stride=rows), :] = product[:, t * LANES : (t + 1) * LANES]
    tiles[...] = staged[...].reshape(tiles.shape).astype(jnp.bfloat16)
    tiles_done = [
        send(tiles.at[wide_at[m], narrow_at[k]], tiles_all.at[n, w], wide_at[m], narrow_at[k])
        for m, k in peers
    ]
    tiles_all[n, w] = tiles[w, n]

    def chunk(k):
        first = z_at[k] * CORES
        wide_rows = jnp.concatenate([trial[first + p] for p in range(CORES)], axis=1)
        return lax.dot_general(
            wide_rows, virt[k], (((1,), (1,)), ((), ())), preferred_element_type=jnp.float32
        )

    across = {}
    for k in range(1, zs):
        along_z[k].wait_recv()
        block = z_at[k] * CORES + c
        across[k] = [send(share(block, w), share(block, w), wide_at[m], n) for m in wide_order]

    get_virt[0].wait()
    to_mate.wait_recv()
    total[...] = chunk(0)

    relayed = {}
    for k in range(1, zs):
        for copy in across[k]:
            copy.wait_recv()
        block = z_at[k] * CORES + c
        relayed[k] = send(trial.at[block], trial.at[block], w, z * CORES + mate)
    for k in range(1, zs - 1):
        get_virt[k].wait()
        relayed[k].wait_recv()
        total[...] += chunk(k)

    get_virt[zs - 1].wait()
    relayed[zs - 1].wait_recv()
    for copy in tiles_done:
        copy.wait_recv()
    columns = []
    for h in range(halves_j):
        parts = [
            tiles_all[b, a].astype(jnp.float32)[h * own_i : (h + 1) * own_i]
            for a in range(wides)
            for b in range(narrows)
        ]
        columns.append(jnp.concatenate(parts, axis=0))
    screened = jnp.concatenate(columns, axis=1).astype(jnp.bfloat16)

    whole = (total[...] + chunk(zs - 1)).astype(jnp.bfloat16)

    product = jnp.dot(screened, whole, preferred_element_type=jnp.float32)
    for b in range(narrows):
        to_core[b] = product[:, b * LANES : (b + 1) * LANES].astype(jnp.bfloat16)
    order = list(range(zs - 1, -1, -1))
    from_mate, from_wides, from_zs = {}, {}, {}
    for k in order:
        from_mate[k] = send(
            to_core.at[z_at[k] * CORES + mate], from_core.at[k], w, z * CORES + mate
        )
    for b in range(narrows):
        partial[b] = product[:, b * LANES : (b + 1) * LANES]
    early = len(sent)
    for k in order:
        from_mate[k].wait_recv()
        value = partial[z_at[k] * CORES + c] + from_core[k].astype(jnp.float32)
        summed[k] = value
        to_wide[k] = value.astype(jnp.bfloat16)
        from_wides[k] = [
            send(
                to_wide.at[k, pl.ds(pl.multiple_of(wide_at[m] * cut, cut), cut)],
                from_wide.at[k, m - 1], wide_at[m], n,
            )
            for m in wide_order
        ]
    for copy in sent[:early]:
        copy.wait_send()
    for k in order:
        value = summed[k, pl.ds(pl.multiple_of(w * cut, cut), cut), :]
        for copy in from_wides[k]:
            copy.wait_recv()
        for m in range(1, wides):
            value = value + from_wide[k, m - 1].astype(jnp.float32)
        if k:
            to_z[k - 1] = value.astype(jnp.bfloat16)
            from_zs[k] = send(to_z.at[k - 1], from_z.at[k - 1], w, z_at[k] * CORES + c)
    for copy in sent[early : early + zs * (wides - 1)]:
        copy.wait_send()
    for k in range(1, zs):
        from_zs[k].wait_recv()
        value = value + from_z[k - 1].astype(jnp.float32)
    out_ref[...] = value
    for copy in sent[early + zs * (wides - 1) :]:
        copy.wait_send()


def fused(wides, narrows, pair_integrals, screening, virtual_integrals, trials):
    zs = narrows // CORES
    orbitals, columns = trials.shape[1:]
    virtuals = virtual_integrals.shape[1]
    aux = screening.shape[1]
    pairs_here = pair_integrals.shape[0]
    rows = pairs_here // LANES
    cut = orbitals // wides
    bf, f4 = jnp.bfloat16, jnp.float32
    copies = (zs - 1) * 2 + 1 + (zs - 1) * (wides - 1) + (wides * narrows - 1)
    copies += zs + zs * (wides - 1) + (zs - 1)
    anywhere = pl.BlockSpec(memory_space=pl.ANY)
    operands = (pair_integrals.T, screening, virtual_integrals[0], trials[0])
    out = pl.pallas_call(
        functools.partial(kernel, wides, narrows),
        out_shape=jax.ShapeDtypeStruct((cut, columns), f4),
        in_specs=[anywhere] * 4,
        out_specs=pl.BlockSpec(memory_space=pltpu.VMEM),
        scratch_shapes=[
            pltpu.VMEM((aux, pairs_here), bf),
            pltpu.VMEM(screening.shape, bf),
            pltpu.VMEM((zs, virtuals, virtuals // zs), bf),
            pltpu.VMEM((narrows, orbitals, columns), bf),
            pltpu.VMEM((aux * rows, LANES), f4),
            pltpu.VMEM((wides, narrows, rows, LANES), bf),
            pltpu.VMEM((narrows, wides, rows, LANES), bf),
            pltpu.VMEM((orbitals, virtuals), f4),
            pltpu.VMEM((narrows, orbitals, columns), f4),
            pltpu.VMEM((narrows, orbitals, columns), bf),
            pltpu.VMEM((zs, orbitals, columns), bf),
            pltpu.VMEM((zs, orbitals, columns), f4),
            pltpu.VMEM((zs, orbitals, columns), bf),
            pltpu.VMEM((zs, wides - 1, cut, columns), bf),
            pltpu.VMEM((zs - 1, cut, columns), bf),
            pltpu.VMEM((zs - 1, cut, columns), bf),
            pltpu.SemaphoreType.DMA((3 + zs,)),
            pltpu.SemaphoreType.DMA((copies,)),
            pltpu.SemaphoreType.DMA((copies,)),
        ],
        compiler_params=pltpu.CompilerParams(
            collective_id=0, has_side_effects=True, vmem_limit_bytes=32 * 2**20
        ),
    )(*[pltpu.with_memory_space_constraint(x, pltpu.HBM) for x in operands])
    return out.T[:, None, :]


def plain(pair_integrals, screening, virtual_integrals, trials):
    orbitals = trials.shape[1]
    screened = jnp.dot(pair_integrals, screening, preferred_element_type=jnp.float32).astype(
        jnp.bfloat16
    )
    blocks = screened.reshape((1, 1) + screened.shape)
    owned_tiles = lax.all_to_all(
        lax.all_to_all(blocks, "wide", split_axis=3, concat_axis=0, tiled=True),
        "narrow",
        split_axis=3,
        concat_axis=1,
        tiled=True,
    )
    pair_tiles = owned_tiles.reshape(orbitals, orbitals, owned_tiles.shape[3])
    whole_trials = lax.all_gather(trials, "narrow", axis=2, tiled=True)
    halves = jnp.einsum(
        "qab,sjb->qasj", virtual_integrals, whole_trials, preferred_element_type=jnp.float32
    ).astype(jnp.bfloat16)
    shares = lax.psum_scatter(
        jnp.einsum("qasj,ijq->asi", halves, pair_tiles, preferred_element_type=jnp.float32),
        "narrow",
        scatter_dimension=0,
        tiled=True,
    )
    return lax.psum_scatter(shares, "wide", scatter_dimension=2, tiled=True)


def per_device(wides, narrows, pair_integrals, screening, virtual_integrals, trials):
    trial_count, orbitals, columns = trials.shape
    own_i = pair_integrals.shape[0] // orbitals
    fits = (
        trial_count == 1
        and virtual_integrals.shape[0] == 1
        and screening.shape[1] == wides * narrows
        and columns == LANES
        and orbitals % LANES == 0
        and orbitals % (16 * wides) == 0
        and narrows % CORES == 0
        and wides & (wides - 1) == 0
        and narrows & (narrows - 1) == 0
        and wides > 1
        and narrows > CORES
        and own_i % 8 == 0
        and (own_i * orbitals // LANES) % 16 == 0
    )
    if fits:
        return fused(wides, narrows, pair_integrals, screening, virtual_integrals, trials)
    return plain(pair_integrals, screening, virtual_integrals, trials)


def solution(mesh):
    return jax.shard_map(
        functools.partial(per_device, mesh.shape["wide"], mesh.shape["narrow"]),
        mesh=mesh,
        in_specs=(
            P(("wide", "narrow"), None),
            P(),
            P(("wide", "narrow"), None, None),
            P(None, None, "narrow"),
        ),
        out_specs=P("narrow", None, "wide"),
        check_vma=False,
    )
```

```python
import functools

import jax
import jax.numpy as jnp
from jax import lax
from jax.experimental import pallas as pl
from jax.experimental.pallas import tpu as pltpu
from jax.sharding import PartitionSpec as P

LANES = 128
CORES = 2
MESH = pl.DeviceIdType.MESH


def flipped(index, mask):
    bit = 1
    result = index
    while bit <= mask:
        if mask & bit:
            result = result + bit * (1 - 2 * lax.rem(lax.div(index, bit), 2))
        bit *= 2
    return result


def kernel(
    wides, narrows, pairs_ref, screen_ref, virt_ref, trial_ref, out_ref,
    pairs, screen, virt, trial, staged, tiles, tiles_wide, tiles_all, screened, total,
    summed, to_wide, from_wide, to_z, from_z,
    local_sem, send_sem, recv_sem,
):
    zs = narrows // CORES
    w, n = lax.axis_index("wide"), lax.axis_index("narrow")
    z, c = lax.div(n, CORES), lax.rem(n, CORES)
    mate = 1 - c
    orbitals = trial.shape[1]
    cut = orbitals // wides
    wide_at = [flipped(w, m) for m in range(wides)]
    z_at = [flipped(z, k) for k in range(zs)]
    wide_order = [wides - 1] + list(range(1, wides - 1))
    order = list(range(zs - 1, -1, -1))

    barrier = pltpu.get_barrier_semaphore()
    for m in wide_order:
        pl.semaphore_signal(barrier, inc=1, device_id={"wide": wide_at[m], "narrow": n}, device_id_type=MESH)
    for narrow in [z_at[k] * CORES + c for k in range(1, zs)] + [z * CORES + mate]:
        pl.semaphore_signal(barrier, inc=1, device_id={"wide": w, "narrow": narrow}, device_id_type=MESH)

    sent = []

    def send(source, target, wide, narrow):
        at = len(sent)
        copy = pltpu.make_async_remote_copy(
            src_ref=source, dst_ref=target, send_sem=send_sem.at[at], recv_sem=recv_sem.at[at],
            device_id={"wide": wide, "narrow": narrow}, device_id_type=MESH,
        )
        copy.start()
        sent.append(copy)
        return copy

    def to_mate(source, target):
        return send(source, target, w, z * CORES + mate)

    def fetch(source, target, at):
        copy = pltpu.make_async_copy(source, target, local_sem.at[at])
        copy.start()
        return copy

    get_trial = fetch(trial_ref, trial.at[n], 2)
    get_pairs = fetch(pairs_ref, pairs, 0)
    get_screen = fetch(screen_ref, screen, 1)

    pl.semaphore_wait(barrier, wides - 1 + zs)

    def share(block, of):
        return trial.at[block, pl.ds(pl.multiple_of(of * cut, cut), cut)]

    get_trial.wait()
    along_z = {k: send(share(n, w), share(n, w), w, z_at[k] * CORES + c) for k in range(1, zs)}
    own_block = to_mate(trial.at[n], trial.at[n])

    depth = virt.shape[4]

    def rows_for(core, k):
        return virt_ref.at[:, core, :, pl.ds(pl.multiple_of(z_at[k] * depth, depth), depth)]

    get_virt = [fetch(rows_for(c, k), virt.at[k, c], 3 + k) for k in range(zs)]
    mate_virt = [to_mate(rows_for(mate, k), virt.at[k, c]) for k in range(zs)]

    get_pairs.wait()
    get_screen.wait()
    product = lax.dot_general(
        screen[...], pairs[...], (((0,), (0,)), ((), ())), preferred_element_type=jnp.float32
    )
    aux = wides * narrows
    rows = tiles.shape[2]
    halves_j = orbitals // LANES
    own_i = rows // halves_j
    for i in range(own_i):
        for h in range(halves_j):
            t = i * halves_j + h
            staged[pl.ds(h * own_i + i, aux, stride=rows), :] = product[:, t * LANES : (t + 1) * LANES]
    tiles[...] = staged[...].reshape(tiles.shape).astype(jnp.bfloat16)
    tiles_wide[w] = tiles[w]
    tiles_in = [send(tiles.at[wide_at[m]], tiles_wide.at[w], wide_at[m], n) for m in wide_order]

    def chunk(k):
        first = z_at[k] * CORES
        wide_rows = jnp.concatenate([trial[first + p] for p in range(CORES)], axis=1)
        return lax.dot_general(
            wide_rows, virt[k].reshape(-1, depth), (((1,), (1,)), ((), ())),
            preferred_element_type=jnp.float32,
        )

    across = {}
    for k in range(1, zs):
        along_z[k].wait_recv()
        block = z_at[k] * CORES + c
        across[k] = [send(share(block, w), share(block, w), wide_at[m], n) for m in wide_order]

    for copy in tiles_in:
        copy.wait_recv()
    tiles_z = {}
    for k in range(zs - 1, 0, -1):
        source = tiles_wide.at[:, pl.ds(z_at[k] * CORES, CORES)]
        tiles_z[k] = send(source, tiles_all.at[c, :, z], w, z_at[k] * CORES + c)
    tiles_all[c, :, z] = tiles_wide[:, pl.ds(z * CORES, CORES)]

    get_virt[0].wait()
    own_block.wait_recv()
    mate_virt[0].wait_recv()
    total[...] = chunk(0)

    relayed, tiles_done = {}, {}

    def relay_tiles(k):
        if k:
            tiles_z[k].wait_recv()
        group = tiles_all.at[c, :, z_at[k]]
        tiles_done[k] = to_mate(group, group)

    def assemble(k):
        tall = CORES * own_i
        for a in range(wides):
            at = pl.ds(pl.multiple_of((a * zs + z_at[k]) * tall, tall), tall)
            for q in range(CORES):
                parts = [tiles_all[p, a, z_at[k], q].astype(jnp.float32) for p in range(CORES)]
                for h in range(halves_j):
                    both = jnp.concatenate([part[h * own_i : (h + 1) * own_i] for part in parts], axis=0)
                    screened[q, at, h * LANES : (h + 1) * LANES] = both.astype(jnp.bfloat16)

    def arrive(k):
        get_virt[k].wait()
        mate_virt[k].wait_recv()
        relayed[k].wait_recv()

    for k in range(1, zs):
        relay_tiles(zs - k)
        for copy in across[k]:
            copy.wait_recv()
        block = z_at[k] * CORES + c
        relayed[k] = to_mate(trial.at[block], trial.at[block])
        if k == zs - 1:
            relay_tiles(0)
        if k > 1:
            arrive(k - 1)
            tiles_done[zs - k + 1].wait_recv()
            total[...] += chunk(k - 1)
            assemble(zs - k + 1)
    tiles_done[1].wait_recv()
    assemble(1)
    tiles_done[0].wait_recv()
    arrive(zs - 1)
    assemble(0)
    whole = (total[...] + chunk(zs - 1)).astype(jnp.bfloat16)

    span = zs * LANES
    product = sum(
        jnp.dot(screened[q], whole[:, q * span : (q + 1) * span], preferred_element_type=jnp.float32)
        for q in range(CORES)
    )
    for b in range(zs):
        to_wide[b] = product[:, b * LANES : (b + 1) * LANES].astype(jnp.bfloat16)
    from_wides, from_zs = {}, {}
    early = len(sent)
    for k in order:
        from_wides[k] = [
            send(
                to_wide.at[z_at[k], pl.ds(pl.multiple_of(wide_at[m] * cut, cut), cut)],
                from_wide.at[k, m - 1], wide_at[m], n,
            )
            for m in wide_order
        ]
    for b in range(zs):
        summed[b] = product[:, b * LANES : (b + 1) * LANES]
    for copy in sent[:early]:
        copy.wait_send()
    for k in order:
        value = summed[z_at[k], pl.ds(pl.multiple_of(w * cut, cut), cut), :]
        for copy in from_wides[k]:
            copy.wait_recv()
        for m in range(1, wides):
            value = value + from_wide[k, m - 1].astype(jnp.float32)
        if k:
            to_z[k - 1] = value.astype(jnp.bfloat16)
            from_zs[k] = send(to_z.at[k - 1], from_z.at[k - 1], w, z_at[k] * CORES + c)
    for copy in sent[early : early + zs * (wides - 1)]:
        copy.wait_send()
    for k in range(1, zs):
        from_zs[k].wait_recv()
        value = value + from_z[k - 1].astype(jnp.float32)
    out_ref[...] = value
    for copy in sent[early + zs * (wides - 1) :]:
        copy.wait_send()


def fused(wides, narrows, pair_integrals, screening, virtual_integrals, trials):
    zs = narrows // CORES
    orbitals, columns = trials.shape[1:]
    virtuals = virtual_integrals.shape[1]
    aux = screening.shape[1]
    pairs_here = pair_integrals.shape[0]
    rows = pairs_here // LANES
    cut = orbitals // wides
    bf, f4 = jnp.bfloat16, jnp.float32
    copies = (zs - 1) * 2 + 1 + zs + (wides - 1) + (zs - 1) + (zs - 1) * (wides - 1) + zs
    copies += zs * (wides - 1) + (zs - 1)
    anywhere = pl.BlockSpec(memory_space=pl.ANY)
    slabs = virtual_integrals.reshape(zs, CORES, columns, virtuals)
    operands = (pair_integrals.T, screening, slabs, trials[0])
    out = pl.pallas_call(
        functools.partial(kernel, wides, narrows),
        out_shape=jax.ShapeDtypeStruct((cut, columns), f4),
        in_specs=[anywhere] * 4,
        out_specs=pl.BlockSpec(memory_space=pltpu.VMEM),
        scratch_shapes=[
            pltpu.VMEM((aux, pairs_here), bf),
            pltpu.VMEM(screening.shape, bf),
            pltpu.VMEM((zs, CORES, zs, columns, virtuals // zs), bf),
            pltpu.VMEM((narrows, orbitals, columns), bf),
            pltpu.VMEM((aux * rows, LANES), f4),
            pltpu.VMEM((wides, narrows, rows, LANES), bf),
            pltpu.VMEM((wides, narrows, rows, LANES), bf),
            pltpu.VMEM((CORES, wides, zs, CORES, rows, LANES), bf),
            pltpu.VMEM((CORES, orbitals, orbitals), bf),
            pltpu.VMEM((orbitals, virtuals), f4),
            pltpu.VMEM((zs, orbitals, columns), f4),
            pltpu.VMEM((zs, orbitals, columns), bf),
            pltpu.VMEM((zs, wides - 1, cut, columns), bf),
            pltpu.VMEM((zs - 1, cut, columns), bf),
            pltpu.VMEM((zs - 1, cut, columns), bf),
            pltpu.SemaphoreType.DMA((3 + zs,)),
            pltpu.SemaphoreType.DMA((copies,)),
            pltpu.SemaphoreType.DMA((copies,)),
        ],
        compiler_params=pltpu.CompilerParams(
            collective_id=0, has_side_effects=True, vmem_limit_bytes=32 * 2**20
        ),
    )(*[pltpu.with_memory_space_constraint(x, pltpu.HBM) for x in operands])
    return out.T[:, None, :]


def plain(pair_integrals, screening, virtual_integrals, trials):
    orbitals = trials.shape[1]
    screened = jnp.dot(pair_integrals, screening, preferred_element_type=jnp.float32).astype(
        jnp.bfloat16
    )
    blocks = screened.reshape((1, 1) + screened.shape)
    owned_tiles = lax.all_to_all(
        lax.all_to_all(blocks, "wide", split_axis=3, concat_axis=0, tiled=True),
        "narrow",
        split_axis=3,
        concat_axis=1,
        tiled=True,
    )
    pair_tiles = owned_tiles.reshape(orbitals, orbitals, owned_tiles.shape[3])
    whole_trials = lax.all_gather(trials, "narrow", axis=2, tiled=True)
    halves = jnp.einsum(
        "qab,sjb->qasj", virtual_integrals, whole_trials, preferred_element_type=jnp.float32
    ).astype(jnp.bfloat16)
    shares = lax.psum_scatter(
        jnp.einsum("qasj,ijq->asi", halves, pair_tiles, preferred_element_type=jnp.float32),
        "narrow",
        scatter_dimension=0,
        tiled=True,
    )
    return lax.psum_scatter(shares, "wide", scatter_dimension=2, tiled=True)


def per_device(wides, narrows, pair_integrals, screening, virtual_integrals, trials):
    trial_count, orbitals, columns = trials.shape
    own_i = pair_integrals.shape[0] // orbitals
    fits = (
        trial_count == 1
        and virtual_integrals.shape[0] == 1
        and screening.shape[1] == wides * narrows
        and columns == LANES
        and orbitals % LANES == 0
        and orbitals % (16 * wides) == 0
        and narrows % CORES == 0
        and wides & (wides - 1) == 0
        and narrows & (narrows - 1) == 0
        and wides > 1
        and narrows > CORES
        and own_i % 8 == 0
        and (own_i * orbitals // LANES) % 16 == 0
    )
    if fits:
        return fused(wides, narrows, pair_integrals, screening, virtual_integrals, trials)
    return plain(pair_integrals, screening, virtual_integrals, trials)


def solution(mesh):
    return jax.shard_map(
        functools.partial(per_device, mesh.shape["wide"], mesh.shape["narrow"]),
        mesh=mesh,
        in_specs=(
            P(("wide", "narrow"), None),
            P(),
            P(("wide", "narrow"), None, None),
            P(None, None, "narrow"),
        ),
        out_specs=P("narrow", None, "wide"),
        check_vma=False,
    )
```

```python
import functools

import jax
import jax.numpy as jnp
from jax import lax
from jax.experimental import pallas as pl
from jax.experimental.pallas import tpu as pltpu
from jax.sharding import PartitionSpec as P

LANES = 128
CORES = 2
MESH = pl.DeviceIdType.MESH


def flipped(index, mask):
    bit = 1
    result = index
    while bit <= mask:
        if mask & bit:
            result = result + bit * (1 - 2 * lax.rem(lax.div(index, bit), 2))
        bit *= 2
    return result


def kernel(
    wides, narrows, pairs_ref, screen_ref, virt_ref, trial_ref, out_ref,
    pairs, screen, virt, trial, staged, tiles, tiles_wide, tiles_all, total, partial,
    to_core, from_core, summed, to_wide, from_wide, to_z, from_z,
    local_sem, send_sem, recv_sem,
):
    zs = narrows // CORES
    w, n = lax.axis_index("wide"), lax.axis_index("narrow")
    z, c = lax.div(n, CORES), lax.rem(n, CORES)
    mate = 1 - c
    orbitals = trial.shape[1]
    cut = orbitals // wides
    wide_at = [flipped(w, m) for m in range(wides)]
    z_at = [flipped(z, k) for k in range(zs)]
    narrow_at = [flipped(n, m) for m in range(narrows)]
    wide_order = [wides - 1] + list(range(1, wides - 1))

    barrier = pltpu.get_barrier_semaphore()
    for m in range(1, wides):
        pl.semaphore_signal(barrier, inc=1, device_id={"wide": wide_at[m], "narrow": n}, device_id_type=MESH)
    for m in range(1, narrows):
        pl.semaphore_signal(barrier, inc=1, device_id={"wide": w, "narrow": narrow_at[m]}, device_id_type=MESH)

    sent = []

    def send(source, target, wide, narrow):
        at = len(sent)
        copy = pltpu.make_async_remote_copy(
            src_ref=source, dst_ref=target, send_sem=send_sem.at[at], recv_sem=recv_sem.at[at],
            device_id={"wide": wide, "narrow": narrow}, device_id_type=MESH,
        )
        copy.start()
        sent.append(copy)
        return copy

    def fetch(source, target, at):
        copy = pltpu.make_async_copy(source, target, local_sem.at[at])
        copy.start()
        return copy

    get_trial = fetch(trial_ref, trial.at[n], 2)
    get_pairs = fetch(pairs_ref, pairs, 0)
    get_screen = fetch(screen_ref, screen, 1)

    pl.semaphore_wait(barrier, wides + narrows - 2)

    def share(block, of):
        return trial.at[block, pl.ds(pl.multiple_of(of * cut, cut), cut)]

    get_trial.wait()
    along_z = {k: send(share(n, w), share(n, w), w, z_at[k] * CORES + c) for k in range(1, zs)}
    to_mate = send(trial.at[n], trial.at[n], w, z * CORES + mate)
    depth = virt.shape[2]
    get_virt = [
        fetch(virt_ref.at[:, pl.ds(pl.multiple_of(z_at[k] * depth, depth), depth)], virt.at[k], 3 + k)
        for k in range(zs)
    ]

    get_pairs.wait()
    get_screen.wait()
    product = lax.dot_general(
        screen[...], pairs[...], (((0,), (0,)), ((), ())), preferred_element_type=jnp.float32
    )
    aux = wides * narrows
    rows = tiles.shape[2]
    halves_j = orbitals // LANES
    own_i = rows // halves_j
    for i in range(own_i):
        for h in range(halves_j):
            t = i * halves_j + h
            staged[pl.ds(h * own_i + i, aux, stride=rows), :] = product[:, t * LANES : (t + 1) * LANES]
    tiles[...] = staged[...].reshape(tiles.shape).astype(jnp.bfloat16)
    tiles_wide[w] = tiles[w]
    tiles_in = [send(tiles.at[wide_at[m]], tiles_wide.at[w], wide_at[m], n) for m in wide_order]

    def chunk(k):
        first = z_at[k] * CORES
        wide_rows = jnp.concatenate([trial[first + p] for p in range(CORES)], axis=1)
        return lax.dot_general(
            wide_rows, virt[k], (((1,), (1,)), ((), ())), preferred_element_type=jnp.float32
        )

    for copy in tiles_in:
        copy.wait_recv()
    tiles_all[n] = tiles_wide[:, n]
    tiles_done = [
        send(tiles_wide.at[:, narrow_at[m]], tiles_all.at[n], w, narrow_at[m])
        for m in range(narrows - 1, 0, -1)
    ]

    across = {}
    for k in range(1, zs):
        along_z[k].wait_recv()
        block = z_at[k] * CORES + c
        across[k] = [send(share(block, w), share(block, w), wide_at[m], n) for m in wide_order]

    get_virt[0].wait()
    to_mate.wait_recv()
    total[...] = chunk(0)

    relayed = {}
    for k in range(1, zs):
        for copy in across[k]:
            copy.wait_recv()
        block = z_at[k] * CORES + c
        relayed[k] = send(trial.at[block], trial.at[block], w, z * CORES + mate)
    for k in range(1, zs - 1):
        get_virt[k].wait()
        relayed[k].wait_recv()
        total[...] += chunk(k)

    get_virt[zs - 1].wait()
    relayed[zs - 1].wait_recv()
    for copy in tiles_done:
        copy.wait_recv()
    columns = []
    for h in range(halves_j):
        parts = [
            tiles_all[b, a].astype(jnp.float32)[h * own_i : (h + 1) * own_i]
            for a in range(wides)
            for b in range(narrows)
        ]
        columns.append(jnp.concatenate(parts, axis=0))
    screened = jnp.concatenate(columns, axis=1).astype(jnp.bfloat16)

    whole = (total[...] + chunk(zs - 1)).astype(jnp.bfloat16)

    product = jnp.dot(screened, whole, preferred_element_type=jnp.float32)
    for b in range(narrows):
        to_core[b] = product[:, b * LANES : (b + 1) * LANES].astype(jnp.bfloat16)
    order = list(range(zs - 1, -1, -1))
    from_mate, from_wides, from_zs = {}, {}, {}
    for k in order:
        from_mate[k] = send(
            to_core.at[z_at[k] * CORES + mate], from_core.at[k], w, z * CORES + mate
        )
    for b in range(narrows):
        partial[b] = product[:, b * LANES : (b + 1) * LANES]
    early = len(sent)
    for k in order:
        from_mate[k].wait_recv()
        value = partial[z_at[k] * CORES + c] + from_core[k].astype(jnp.float32)
        summed[k] = value
        to_wide[k] = value.astype(jnp.bfloat16)
        from_wides[k] = [
            send(
                to_wide.at[k, pl.ds(pl.multiple_of(wide_at[m] * cut, cut), cut)],
                from_wide.at[k, m - 1], wide_at[m], n,
            )
            for m in wide_order
        ]
    for copy in sent[:early]:
        copy.wait_send()
    for k in order:
        value = summed[k, pl.ds(pl.multiple_of(w * cut, cut), cut), :]
        for copy in from_wides[k]:
            copy.wait_recv()
        for m in range(1, wides):
            value = value + from_wide[k, m - 1].astype(jnp.float32)
        if k:
            to_z[k - 1] = value.astype(jnp.bfloat16)
            from_zs[k] = send(to_z.at[k - 1], from_z.at[k - 1], w, z_at[k] * CORES + c)
    for copy in sent[early : early + zs * (wides - 1)]:
        copy.wait_send()
    for k in range(1, zs):
        from_zs[k].wait_recv()
        value = value + from_z[k - 1].astype(jnp.float32)
    out_ref[...] = value
    for copy in sent[early + zs * (wides - 1) :]:
        copy.wait_send()


def fused(wides, narrows, pair_integrals, screening, virtual_integrals, trials):
    zs = narrows // CORES
    orbitals, columns = trials.shape[1:]
    virtuals = virtual_integrals.shape[1]
    aux = screening.shape[1]
    pairs_here = pair_integrals.shape[0]
    rows = pairs_here // LANES
    cut = orbitals // wides
    bf, f4 = jnp.bfloat16, jnp.float32
    copies = (zs - 1) * 2 + 1 + (zs - 1) * (wides - 1) + (wides - 1) + (narrows - 1)
    copies += zs + zs * (wides - 1) + (zs - 1)
    anywhere = pl.BlockSpec(memory_space=pl.ANY)
    operands = (pair_integrals.T, screening, virtual_integrals[0], trials[0])
    out = pl.pallas_call(
        functools.partial(kernel, wides, narrows),
        out_shape=jax.ShapeDtypeStruct((cut, columns), f4),
        in_specs=[anywhere] * 4,
        out_specs=pl.BlockSpec(memory_space=pltpu.VMEM),
        scratch_shapes=[
            pltpu.VMEM((aux, pairs_here), bf),
            pltpu.VMEM(screening.shape, bf),
            pltpu.VMEM((zs, virtuals, virtuals // zs), bf),
            pltpu.VMEM((narrows, orbitals, columns), bf),
            pltpu.VMEM((aux * rows, LANES), f4),
            pltpu.VMEM((wides, narrows, rows, LANES), bf),
            pltpu.VMEM((wides, narrows, rows, LANES), bf),
            pltpu.VMEM((narrows, wides, rows, LANES), bf),
            pltpu.VMEM((orbitals, virtuals), f4),
            pltpu.VMEM((narrows, orbitals, columns), f4),
            pltpu.VMEM((narrows, orbitals, columns), bf),
            pltpu.VMEM((zs, orbitals, columns), bf),
            pltpu.VMEM((zs, orbitals, columns), f4),
            pltpu.VMEM((zs, orbitals, columns), bf),
            pltpu.VMEM((zs, wides - 1, cut, columns), bf),
            pltpu.VMEM((zs - 1, cut, columns), bf),
            pltpu.VMEM((zs - 1, cut, columns), bf),
            pltpu.SemaphoreType.DMA((3 + zs,)),
            pltpu.SemaphoreType.DMA((copies,)),
            pltpu.SemaphoreType.DMA((copies,)),
        ],
        compiler_params=pltpu.CompilerParams(
            collective_id=0, has_side_effects=True, vmem_limit_bytes=32 * 2**20
        ),
    )(*[pltpu.with_memory_space_constraint(x, pltpu.HBM) for x in operands])
    return out.T[:, None, :]


def plain(pair_integrals, screening, virtual_integrals, trials):
    orbitals = trials.shape[1]
    screened = jnp.dot(pair_integrals, screening, preferred_element_type=jnp.float32).astype(
        jnp.bfloat16
    )
    blocks = screened.reshape((1, 1) + screened.shape)
    owned_tiles = lax.all_to_all(
        lax.all_to_all(blocks, "wide", split_axis=3, concat_axis=0, tiled=True),
        "narrow",
        split_axis=3,
        concat_axis=1,
        tiled=True,
    )
    pair_tiles = owned_tiles.reshape(orbitals, orbitals, owned_tiles.shape[3])
    whole_trials = lax.all_gather(trials, "narrow", axis=2, tiled=True)
    halves = jnp.einsum(
        "qab,sjb->qasj", virtual_integrals, whole_trials, preferred_element_type=jnp.float32
    ).astype(jnp.bfloat16)
    shares = lax.psum_scatter(
        jnp.einsum("qasj,ijq->asi", halves, pair_tiles, preferred_element_type=jnp.float32),
        "narrow",
        scatter_dimension=0,
        tiled=True,
    )
    return lax.psum_scatter(shares, "wide", scatter_dimension=2, tiled=True)


def per_device(wides, narrows, pair_integrals, screening, virtual_integrals, trials):
    trial_count, orbitals, columns = trials.shape
    own_i = pair_integrals.shape[0] // orbitals
    fits = (
        trial_count == 1
        and virtual_integrals.shape[0] == 1
        and screening.shape[1] == wides * narrows
        and columns == LANES
        and orbitals % LANES == 0
        and orbitals % (16 * wides) == 0
        and narrows % CORES == 0
        and wides & (wides - 1) == 0
        and narrows & (narrows - 1) == 0
        and wides > 1
        and narrows > CORES
        and own_i % 8 == 0
        and (own_i * orbitals // LANES) % 16 == 0
    )
    if fits:
        return fused(wides, narrows, pair_integrals, screening, virtual_integrals, trials)
    return plain(pair_integrals, screening, virtual_integrals, trials)


def solution(mesh):
    return jax.shard_map(
        functools.partial(per_device, mesh.shape["wide"], mesh.shape["narrow"]),
        mesh=mesh,
        in_specs=(
            P(("wide", "narrow"), None),
            P(),
            P(("wide", "narrow"), None, None),
            P(None, None, "narrow"),
        ),
        out_specs=P("narrow", None, "wide"),
        check_vma=False,
    )
```
